256 devices in a mesh: ctx: 32 (over z, x_hi, core), head: 8 (over y, x_lo).
Axes of the slice: x: 4 (x_hi: 2, x_lo: 2; x = x_hi * 2 + x_lo), y: 4, z: 8, core: 2. Of those that a mesh axis runs over, the one named last changes fastest.
Arguments:
- queries: float32 [512, 8, 2048], P('ctx', 'head'), may hold values from -80 to 80
- new_kv: float32 [2, 512, 8, 128], P(None, 'ctx', 'head'), may hold values from -24 to 24
- cache_keys: float32 [4, 32768, 8, 128], P(None, 'ctx', 'head'), may hold values from -4 to 4
- cache_values: float32 [4, 32768, 8, 128], P(None, 'ctx', 'head'), may hold values from -24 to 24
- new_lengths: int32 [4], replicated, may hold values from 1 to 192, 512 in all
- block_plan: int32 [128], P('ctx'), may hold values from 0 to 127, each once
Outputs:
- attended: float32 [512, 16384], P(('ctx', 'head'))
The draws below stay inside these ranges and needn't reach their ends.
Inputs may be any that keep to these rules, and one draw needn't show every extreme that they name: `new_lengths`: the lengths sum to 512 and the largest is exactly 192. `block_plan`: every block number appears once.
All inputs are finite; a program needn't handle non-finite values.
Results may differ from the reference program's by a relative error of at most 0.0003.
Values sent between devices are 32-bit elements; how exact they have to be, the bound alone decides.
No kernel may reach another device: no remote copies, remote signals or barrier semaphores. Data moves between devices by JAX's collectives and lax.ppermute only.
A program may use at most 128 MiB of HBM per device.

```python
import math
import jax
import jax.numpy as jnp
import numpy as np
from jax import lax

HD = 128
QH = 16
REQS = 4
BLOCK = 4
CACHE_DEV = 1024
KVH = 8
NEW_TOTAL = 512
NBLOCKS = 128
CACHE = 32768
MOST = 192


def fresh_keys(key):
    noise = jnp.clip(jax.random.normal(jax.random.fold_in(key, 43), (NEW_TOTAL, KVH, HD), jnp.float32), -4.0, 4.0)
    return noise


def draw_queries(key, part):
    keys = fresh_keys(key)
    key = jax.random.fold_in(key, 5)
    first = jax.random.fold_in(key, 0)
    drawn = jnp.clip(1.5 * jax.random.normal(first, (NEW_TOTAL, KVH, QH, HD), jnp.float32), -6.0, 6.0)
    result = drawn + 0.85 * keys[:, :, None, :]
    return result.reshape(NEW_TOTAL, KVH, QH * HD)


def draw_new_kv(key, part):
    keys = fresh_keys(key)
    key = jax.random.fold_in(key, 9)
    values = 6.0 * jnp.clip(jax.random.normal(key, (NEW_TOTAL, KVH, HD), jnp.float32), -4.0, 4.0)
    return jnp.stack([keys, values])


def levels(own_key, extent, cuts, smallest, top_value):
    loudness = 1.0
    for dim, shards_of in cuts:
        steps = jax.random.uniform(jax.random.fold_in(jax.random.fold_in(own_key, 6), dim), (shards_of,), jnp.float32, smallest / len(cuts), top_value / len(cuts))
        loudness = loudness * jnp.repeat(jnp.exp(steps), extent[dim] // shards_of).reshape((-1,) + (1,) * (len(extent) - 1 - dim))
    return loudness


def length_profile(number_of, total, limit, skew):
    loads = [(1 << 20) // math.isqrt(grade ** skew) + 1 for grade in range(2, number_of + 1)]
    spare, given = total - limit - (number_of - 1), [1] * (number_of - 1)
    while spare > 0:
        candidates = [i for i in range(number_of - 1) if given[i] < limit]
        whole, left = sum([loads[i] for i in candidates]), spare
        for i in candidates:
            extra = min(limit - given[i], max(1, left * loads[i] // whole), spare)
            given[i] = given[i] + extra
            spare = spare - extra
    return np.array([limit] + given)


def ragged(own_key, count, total, reach, slope):
    if count == 2:
        one = jax.random.randint(own_key, (), max(1, total - reach), min(reach, total - 1) + 1)
        return jnp.stack([one, total - one])
    lengths = jnp.asarray(length_profile(count, total, reach, slope), jnp.int32)
    couples = (count - 1) // 2
    giver, sink = lengths[1:1 + 2 * couples:2], lengths[2:2 + 2 * couples:2]
    room = jnp.minimum(giver - 1, reach - sink)
    passed = jax.random.randint(jax.random.fold_in(own_key, 1), (couples,), 0, 1 << 20) % (room + 1)
    lengths = lengths.at[1:1 + 2 * couples:2].set(giver - passed).at[2:2 + 2 * couples:2].set(sink + passed)
    return lengths[jax.random.permutation(jax.random.fold_in(own_key, 2), count)]


def gaussian(rng, dims, width, limit, cuts=(), kind=jnp.bfloat16):
    drawn = width * jax.random.normal(rng, dims, jnp.float32)
    if cuts:
        drawn = drawn * levels(rng, dims, cuts, -0.22, 0.18)
    return jnp.clip(drawn, -limit, limit).astype(kind)


def setup_inputs(seed: int = 0) -> dict:
    arg_keys = jax.random.split(jax.random.key(seed), 7)
    return {
        "queries": draw_queries(jax.random.fold_in(arg_keys[6], 71), 0),
        "new_kv": draw_new_kv(jax.random.fold_in(arg_keys[6], 71), 0),
        "cache_keys": gaussian(arg_keys[2], (REQS, CACHE, KVH, HD), 1.0, 4.0, ((1, 32), (2, 8)), jnp.float32),
        "cache_values": gaussian(arg_keys[3], (REQS, CACHE, KVH, HD), 6.0, 24.0, ((1, 32), (2, 8)), jnp.float32),
        "new_lengths": ragged(arg_keys[4], REQS, NEW_TOTAL, MOST, 2).astype(jnp.int32),
        "block_plan": jax.random.permutation(arg_keys[5], NBLOCKS).astype(jnp.int32),
    }


HIGHEST = lax.Precision.HIGHEST
NEG_FLOOR = -1.0e30


def partial_scores(query_rows, keys, values, allowed):
    scores = jnp.dot(query_rows, keys.T, precision=HIGHEST, preferred_element_type=jnp.float32) * (keys.shape[1] ** -0.5)
    scores = jnp.where(allowed, scores, NEG_FLOOR)
    peak = jnp.max(scores, axis=1)
    weights = jnp.where(allowed, jnp.exp(scores - peak[:, None]), 0.0)
    total = jnp.sum(weights, axis=1)
    summed = jnp.dot(weights, values, precision=HIGHEST, preferred_element_type=jnp.float32)
    return peak, total, summed


def combine(first, second):
    peak = jnp.maximum(first[0], second[0])
    left = jnp.exp(first[0] - peak)
    right = jnp.exp(second[0] - peak)
    return peak, first[1] * left + second[1] * right, first[2] * left[:, None] + second[2] * right[:, None]


def reference(queries, new_kv, cache_keys, cache_values, new_lengths, block_plan):
    rows = jnp.arange(NEW_TOTAL, dtype=jnp.int32)
    packed = (block_plan[rows // BLOCK] * BLOCK + rows % BLOCK).astype(jnp.int32)
    ends = jnp.cumsum(new_lengths).astype(jnp.int32)
    starts = (ends - new_lengths).astype(jnp.int32)
    request = jnp.sum((packed[:, None] >= ends[None, :]).astype(jnp.int32), axis=1).astype(jnp.int32)
    onehot = (request[:, None] == jnp.arange(REQS, dtype=jnp.int32)[None, :]).astype(jnp.int32)
    position = (packed - jnp.sum(onehot * starts[None, :], axis=1)).astype(jnp.int32)
    row_of = jnp.zeros((NEW_TOTAL,), jnp.int32).at[packed].set(rows)
    padded_q = jnp.concatenate([queries[row_of], jnp.zeros((MOST, KVH, QH * HD), queries.dtype)], axis=0)
    padded_kv = jnp.concatenate([new_kv[:, row_of], jnp.zeros((2, MOST, KVH, HD), new_kv.dtype)], axis=1)
    local = jnp.arange(MOST, dtype=jnp.int32)

    def one_request(req):
        start = starts[req]
        live = local < new_lengths[req]
        causal = (local[None, :] <= local[:, None]) & live[None, :]
        causal_rows = jnp.repeat(causal, QH, axis=0)
        q_req = lax.dynamic_slice_in_dim(padded_q, start, MOST, 0)
        kv_req = lax.dynamic_slice_in_dim(padded_kv, start, MOST, 1)
        chat_keys = cache_keys[req]
        chat_values = cache_values[req]

        def one_head(head):
            q_rows = q_req[:, head].reshape(MOST * QH, HD)
            fresh = partial_scores(q_rows, kv_req[0, :, head], kv_req[1, :, head], causal_rows)

            def step(carry, index):
                base = (index * CACHE_DEV).astype(jnp.int32)
                keys = lax.dynamic_slice_in_dim(chat_keys, base, CACHE_DEV, 0)[:, head]
                values = lax.dynamic_slice_in_dim(chat_values, base, CACHE_DEV, 0)[:, head]
                return combine(carry, partial_scores(q_rows, keys, values, True)), None

            final, unused = lax.scan(step, fresh, jnp.arange(CACHE // CACHE_DEV, dtype=jnp.int32))
            return (final[2] / final[1][:, None]).reshape(MOST, QH * HD)

        return lax.map(one_head, jnp.arange(KVH, dtype=jnp.int32))

    results = lax.map(one_request, jnp.arange(REQS, dtype=jnp.int32))
    attended = results[request, :, position]
    return attended.reshape(NEW_TOTAL, KVH * QH * HD)
```

```python
import functools
import math

import jax
import jax.numpy as jnp
from jax import lax
from jax.experimental import pallas as pl
from jax.experimental.pallas import tpu as pltpu
from jax.sharding import PartitionSpec as P

REQS = 4
HD = 128
HEADS = 8
TOK = 16
BLOCK = 4
TOTAL = 512
NBLOCKS = TOTAL // BLOCK
TILE = 32
COLS = TILE * HEADS
POSITIONS = 2048
CHUNK = 512
CHUNKS = POSITIONS // CHUNK
FRESH = 2 * TOK
SLOTS = 16
SLOT_TOK = TOTAL // SLOTS
MAX_TILES = TOTAL // TILE + REQS
NEG = -1e30
SCALE = HD ** (-0.5) * math.log2(math.e)
NT = (((1,), (1,)), ((), ()))
OFFSETS = (0, -1, 1, -2, 2, -3, 3)


def split(x):
    high = x.astype(jnp.bfloat16)
    low = (x - high.astype(jnp.float32)).astype(jnp.bfloat16)
    return high, low


def prepare_kernel(own_k, other_k, own_v, other_v, keys, values):
    half = POSITIONS // 2
    for place, (k, v) in enumerate(((own_k, own_v), (other_k, other_v))):
        rows = pl.ds(place * half, half)
        high, low = split(k[0])
        keys[0, rows, 0:HD] = high
        keys[0, rows, HD : 2 * HD] = high
        keys[0, rows, 2 * HD : 3 * HD] = low
        high, low = split(v[0].T)
        values[0, 0:HD, rows] = high
        values[0, HD : 2 * HD, rows] = low


def prepare(own_k, other_k, own_v, other_v):
    half = POSITIONS // 2
    source = pl.BlockSpec((1, half, HD), lambda r: (r, 0, 0))
    return pl.pallas_call(
        prepare_kernel,
        grid=(REQS,),
        in_specs=[source] * 4,
        out_specs=[
            pl.BlockSpec((1, POSITIONS, 3 * HD), lambda r: (r, 0, 0)),
            pl.BlockSpec((1, 2 * HD, POSITIONS), lambda r: (r, 0, 0)),
        ],
        out_shape=[
            jax.ShapeDtypeStruct((REQS, POSITIONS, 3 * HD), jnp.bfloat16),
            jax.ShapeDtypeStruct((REQS, 2 * HD, POSITIONS), jnp.bfloat16),
        ],
        compiler_params=pltpu.CompilerParams(vmem_limit_bytes=40 << 20),
        cost_estimate=pl.CostEstimate(flops=10**7, bytes_accessed=16 << 20, transcendentals=0),
        name="prepare",
    )(own_k, other_k, own_v, other_v)


def attend_kernel(
    lengths, plan, place, *refs
):
    pieces, refs = refs[:9], refs[9:]
    fresh_own, fresh_other, keys_hbm, values_hbm, out = refs[:5]
    (
        queries, keys, values, fresh_keys, fresh_values, fresh_packed,
        weights, rows, scores_a, scores_b, new_a, new_b, peak_a, peak_b,
        placed, tile_req, tile_first, tile_start, tile_last, sems, kv_sems,
    ) = refs[5:]
    me = place[0]
    z = me // 4
    corner = lax.rem(me, 4)

    copies = []
    for index, piece in enumerate(pieces):
        offset = OFFSETS[index] if index < 7 else 4
        source_z = lax.rem(z + offset + 8, 8)
        for part in range(piece.shape[0] // TOK):
            which = part + (2 if index == 8 else 0)
            target = source_z * 4 + jnp.bitwise_xor(which, corner)
            copies.append(
                pltpu.make_async_copy(
                    piece.at[pl.ds(part * TOK, TOK)],
                    queries.at[pl.ds(target * TOK, TOK)],
                    sems.at[len(copies)],
                )
            )
    for copy in copies:
        copy.start()

    def kv_copies(req):
        return (
            pltpu.make_async_copy(keys_hbm.at[req], keys.at[req], kv_sems.at[req, 0]),
            pltpu.make_async_copy(values_hbm.at[req], values.at[req], kv_sems.at[req, 1]),
        )

    for req in range(REQS):
        for copy in kv_copies(req):
            copy.start()

    def place_block(j, _):
        placed[plan[j]] = j
        return 0

    lax.fori_loop(0, NBLOCKS, place_block, 0)

    begin = jnp.int32(0)
    tiles = jnp.int32(0)
    for req in range(REQS):
        end = begin + lengths[req]
        count = (lengths[req] + TILE - 1) // TILE

        def list_tile(t, _, req=req, begin=begin, end=end, tiles=tiles):
            tile_req[tiles + t] = req
            tile_first[tiles + t] = begin
            tile_start[tiles + t] = begin + t * TILE
            tile_last[tiles + t] = end - 1
            return 0

        lax.fori_loop(0, count, list_tile, 0)
        begin = end
        tiles = tiles + count

    for half, fresh in enumerate((fresh_own, fresh_other)):
        span = pl.ds(half * TOK, TOK)
        high, low = split(fresh[0])
        fresh_keys[span, 0:HD] = high
        fresh_keys[span, HD : 2 * HD] = high
        fresh_keys[span, 2 * HD : 3 * HD] = low
        holder = jnp.bitwise_xor(me, half)
        for u in range(TOK):
            number = plan[holder * (TOK // BLOCK) + u // BLOCK] * BLOCK + u % BLOCK
            fresh_packed[half * TOK + u : half * TOK + u + 1, :] = jnp.full((1, COLS), number, jnp.int32)
    high, low = split(jnp.concatenate([fresh_own[1], fresh_other[1]], axis=0).T)
    fresh_values[0:HD] = high
    fresh_values[HD : 2 * HD] = low

    out[...] = jnp.zeros_like(out)
    for copy in copies:
        copy.wait()

    lane = lax.broadcasted_iota(jnp.int32, (1, COLS), 1) // HEADS
    lanes = lax.broadcasted_iota(jnp.int32, (HEADS, HD), 1)

    def row_of(index, t):
        packed = jnp.minimum(tile_start[index] + t, tile_last[index])
        return placed[packed // BLOCK] * BLOCK + lax.rem(packed, BLOCK)

    def load(index):
        for t in range(TILE):
            rows[pl.ds(t * HEADS, HEADS), :] = queries[row_of(index, t)]
        high, low = split(rows[...] * SCALE)
        weights[:, 0:HD] = high
        weights[:, HD : 2 * HD] = low
        weights[:, 2 * HD : 3 * HD] = high

    def arrive(index):
        req = tile_req[index]

        @pl.when(tile_start[index] == tile_first[index])
        def _():
            for copy in kv_copies(req):
                copy.wait()

    def score_chunk(index, c, scores, peak):
        part = lax.dot_general(
            keys[tile_req[index], pl.ds(c * CHUNK, CHUNK), :], weights[...], NT,
            preferred_element_type=jnp.float32,
        )
        scores[pl.ds(c * CHUNK, CHUNK), :] = part
        top = jnp.max(part.reshape(CHUNK // 8, 8, COLS), axis=0)
        return top if peak is None else jnp.maximum(peak, top)

    def score_fresh(index, new, peak):
        part = lax.dot_general(
            fresh_keys[...], weights[...], NT, preferred_element_type=jnp.float32
        )
        number = fresh_packed[...]
        latest = jnp.minimum(tile_start[index] + lane, tile_last[index])
        allowed = (number >= tile_first[index]) & (number <= latest)
        part = jnp.where(allowed, part, NEG)
        new[...] = part
        return jnp.maximum(peak, jnp.max(part.reshape(FRESH // 8, 8, COLS), axis=0))

    def weigh(part, top):
        p = jnp.exp2(part - top)
        high, low = split(p)
        return jnp.sum(p.reshape(part.shape[0] // 8, 8, COLS), axis=0), high, low

    def accumulate(value, high, low, acc):
        first = jnp.dot(value, high, preferred_element_type=jnp.float32)
        second = jnp.dot(value[0:HD], low, preferred_element_type=jnp.float32)
        both = first[0:HD] + first[HD : 2 * HD] + second
        return both if acc is None else acc + both

    def finish(index, top, mass, acc):
        total = jnp.sum(mass, axis=0, keepdims=True)
        done = (acc / total).T
        level = jnp.broadcast_to(top + jnp.log2(total), (HD, COLS)).T
        for t in range(TILE):
            row = row_of(index, t)
            slot = row // SLOT_TOK
            inside = lax.rem(row, SLOT_TOK)
            out[slot, inside] = done[t * HEADS : (t + 1) * HEADS]
            out[slot, SLOT_TOK] = jnp.where(
                lanes == inside, level[t * HEADS : (t + 1) * HEADS], out[slot, SLOT_TOK]
            )

    def step(now, later, scores_now, new_now, peak_now, scores_later, new_later, peak_later):
        load(later)
        top = jnp.max(peak_now[...], axis=0, keepdims=True)
        mass, high, low = weigh(new_now[...], top)
        acc = accumulate(fresh_values[...], high, low, None)
        peak = None
        for c in range(CHUNKS):
            peak = score_chunk(later, c, scores_later, peak)
            more, high, low = weigh(scores_now[pl.ds(c * CHUNK, CHUNK), :], top)
            mass = mass + more
            acc = accumulate(
                values[tile_req[now], :, pl.ds(c * CHUNK, CHUNK)], high, low, acc
            )
        peak_later[...] = score_fresh(later, new_later, peak)
        finish(now, top, mass, acc)

    arrive(0)
    load(0)
    peak = None
    for c in range(CHUNKS):
        peak = score_chunk(0, c, scores_a, peak)
    peak_a[...] = score_fresh(0, new_a, peak)

    def pair(j, _):
        now = 2 * j
        for this, (a, b) in enumerate(
            (
                ((scores_a, new_a, peak_a), (scores_b, new_b, peak_b)),
                ((scores_b, new_b, peak_b), (scores_a, new_a, peak_a)),
            )
        ):
            current = now + this
            following = jnp.minimum(current + 1, tiles - 1)

            @pl.when(current < tiles)
            def _():
                @pl.when(current + 1 < tiles)
                def _():
                    arrive(following)

                step(current, following, *a, *b)

        return 0

    lax.fori_loop(0, (tiles + 1) // 2, pair, 0)


def attend(lengths, plan, place, pieces, fresh_own, fresh_other, keys, values):
    smem = pl.BlockSpec(memory_space=pltpu.SMEM)
    vmem = pl.BlockSpec(memory_space=pltpu.VMEM)
    hbm = pl.BlockSpec(memory_space=pl.ANY)
    return pl.pallas_call(
        attend_kernel,
        in_specs=[smem] * 3 + [hbm] * 9 + [vmem] * 2 + [hbm] * 2,
        out_specs=vmem,
        out_shape=jax.ShapeDtypeStruct((SLOTS, SLOT_TOK + 1, HEADS, HD), jnp.float32),
        scratch_shapes=[
            pltpu.VMEM((TOTAL, HEADS, HD), jnp.float32),
            pltpu.VMEM((REQS, POSITIONS, 3 * HD), jnp.bfloat16),
            pltpu.VMEM((REQS, 2 * HD, POSITIONS), jnp.bfloat16),
            pltpu.VMEM((FRESH, 3 * HD), jnp.bfloat16),
            pltpu.VMEM((2 * HD, FRESH), jnp.bfloat16),
            pltpu.VMEM((FRESH, COLS), jnp.int32),
            pltpu.VMEM((COLS, 3 * HD), jnp.bfloat16),
            pltpu.VMEM((COLS, HD), jnp.float32),
            pltpu.VMEM((POSITIONS, COLS), jnp.float32),
            pltpu.VMEM((POSITIONS, COLS), jnp.float32),
            pltpu.VMEM((FRESH, COLS), jnp.float32),
            pltpu.VMEM((FRESH, COLS), jnp.float32),
            pltpu.VMEM((8, COLS), jnp.float32),
            pltpu.VMEM((8, COLS), jnp.float32),
            pltpu.SMEM((NBLOCKS,), jnp.int32),
            pltpu.SMEM((MAX_TILES,), jnp.int32),
            pltpu.SMEM((MAX_TILES,), jnp.int32),
            pltpu.SMEM((MAX_TILES,), jnp.int32),
            pltpu.SMEM((MAX_TILES,), jnp.int32),
            pltpu.SemaphoreType.DMA((32,)),
            pltpu.SemaphoreType.DMA((REQS, 2)),
        ],
        compiler_params=pltpu.CompilerParams(vmem_limit_bytes=48 << 20),
        cost_estimate=pl.CostEstimate(
            flops=34 * 10**9, bytes_accessed=14 << 20, transcendentals=10**7
        ),
        name="attend",
    )(lengths, plan, place, *pieces, fresh_own, fresh_other, keys, values)


def merge_kernel(parts, out):
    level = parts[:, SLOT_TOK]
    top = jnp.max(level, axis=0)
    share = jnp.exp2(level - top[None])
    share = share / jnp.sum(share, axis=0)[None]
    for t in range(SLOT_TOK):
        acc = parts[0, t] * share[0][:, t : t + 1]
        for c in range(1, SLOTS):
            acc = acc + parts[c, t] * share[c][:, t : t + 1]
        out[t] = acc


def merge(parts):
    return pl.pallas_call(
        merge_kernel,
        out_shape=jax.ShapeDtypeStruct((SLOT_TOK, HEADS, HD), jnp.float32),
        compiler_params=pltpu.CompilerParams(vmem_limit_bytes=24 << 20),
        name="merge",
    )(parts)


def body(queries, new_kv, cache_keys, cache_values, new_lengths, block_plan):
    me = lax.axis_index("ctx")
    core = me % 2
    n_ctx = 32
    n_head = 8

    def send(x, target):
        return lax.ppermute(x, "ctx", [(i, target(i)) for i in range(n_ctx)])

    def across(i):
        return i ^ 1

    def up(i):
        return (i + 4) % n_ctx

    def down(i):
        return (i - 4) % n_ctx

    q = queries.reshape(TOK, 2, HEADS, HD)
    mine = lax.dynamic_index_in_dim(q, core, 1, keepdims=False)
    theirs = lax.dynamic_index_in_dim(q, 1 - core, 1, keepdims=False)
    own = jnp.concatenate(
        [mine, send(theirs, across), send(mine, lambda i: i ^ 2), send(theirs, lambda i: i ^ 3)],
        axis=0,
    )
    plan = lax.all_to_all(
        jnp.broadcast_to(block_plan[None], (n_ctx,) + block_plan.shape),
        "ctx", split_axis=0, concat_axis=0, tiled=True,
    ).reshape(NBLOCKS)
    keys, values = prepare(
        cache_keys[:, :, 0], send(cache_keys, across)[:, :, 0],
        cache_values[:, :, 0], send(cache_values, across)[:, :, 0],
    )
    fresh = new_kv[:, :, 0]
    fresh_other = send(fresh, across)
    rising, falling = [own], [own]
    for _ in range(3):
        rising.append(send(rising[-1], up))
        falling.append(send(falling[-1], down))
    pieces = [own]
    for k in range(1, 4):
        pieces += [rising[k], falling[k]]
    pieces += [send(rising[3][: 2 * TOK], up), send(falling[3][2 * TOK :], down)]
    parts = attend(new_lengths, plan, me.reshape(1), pieces, fresh, fresh_other, keys, values)
    groups = [[i for i in range(n_ctx) if i % 2 == c] for c in range(2)]
    home = lax.all_to_all(
        parts, "ctx", split_axis=0, concat_axis=0, tiled=True, axis_index_groups=groups
    )
    merged = merge(home).reshape(2, TOK, HEADS, HD)
    keep = lax.dynamic_index_in_dim(merged, core, 0, keepdims=False)
    give = lax.dynamic_index_in_dim(merged, 1 - core, 0, keepdims=False)
    got = send(give, across)
    first = jnp.where(core == 0, keep, got)
    second = jnp.where(core == 0, got, keep)
    wide = jnp.concatenate([first, second], axis=1).reshape(n_head, TOK // n_head, 1, 2 * HEADS * HD)
    regrouped = lax.all_to_all(wide, "head", split_axis=0, concat_axis=2, tiled=True)
    return regrouped.reshape(TOK // n_head, n_head * 2 * HEADS * HD)


def solution(mesh):
    placed = (
        P("ctx", "head", None),
        P(None, "ctx", "head", None),
        P(None, "ctx", "head", None),
        P(None, "ctx", "head", None),
        P(),
        P("ctx"),
    )
    return jax.shard_map(
        body, mesh=mesh, in_specs=placed, out_specs=P(("ctx", "head"), None), check_vma=False
    )
```

```python
import functools
import math

import jax
import jax.numpy as jnp
from jax import lax
from jax.experimental import pallas as pl
from jax.experimental.pallas import tpu as pltpu
from jax.sharding import PartitionSpec as P

REQS = 4
HD = 128
HEADS = 8
TOK = 16
BLOCK = 4
TILE = 32
COLS = TILE * HEADS
POSITIONS = 2048
CHUNK = 512
CHUNKS = POSITIONS // CHUNK
FRESH = 2 * TOK
SLOT_TOK = 2 * TOK
PART = TOK + 1
MEMBER_BLOCKS = 4 * TOK // BLOCK
NBLOCKS = 8 * MEMBER_BLOCKS
TILE_BLOCKS = TILE // BLOCK
MAX_TILES = 12
REACH = (4, 3, -3, 2, -2, 1, -1, 0)
GROUPS = ((0,), (1, 2), (3, 4), (5, 6), (7,))
ROOM = 64
LAST = (len(GROUPS) - 1) * REQS
VMEM = pl.BlockSpec(memory_space=pltpu.VMEM)
SMEM = pl.BlockSpec(memory_space=pltpu.SMEM)
NEG = -1e30
SCALE = HD ** (-0.5) * math.log2(math.e)
NT = (((1,), (1,)), ((), ()))


def split(x):
    high = x.astype(jnp.bfloat16)
    low = (x - high.astype(jnp.float32)).astype(jnp.bfloat16)
    return high, low


def prepare_kernel(
    own_k, other_k, own_v, other_v, fresh_own, fresh_other, message,
    keys, values, fresh_keys, fresh_values, fresh_packed
):
    half = POSITIONS // 2
    for place, (k, v) in enumerate(((own_k, own_v), (other_k, other_v))):
        rows = pl.ds(place * half, half)
        high, low = split(k[0])
        keys[0, rows, 0:HD] = high
        keys[0, rows, HD : 2 * HD] = low
        high, low = split(v[0].T)
        values[0, 0:HD, rows] = high
        values[0, HD : 2 * HD, rows] = low

    @pl.when(pl.program_id(0) == 0)
    def _():
        for half, fresh in enumerate((fresh_own, fresh_other)):
            span = pl.ds(half * TOK, TOK)
            high, low = split(fresh[0])
            fresh_keys[span, 0:HD] = high
            fresh_keys[span, HD : 2 * HD] = low
            plan = message[half * PART + TOK].astype(jnp.int32)
            for u in range(TOK):
                block = plan[0:1, u // BLOCK : u // BLOCK + 1]
                fresh_packed[half * TOK + u : half * TOK + u + 1, :] = jnp.broadcast_to(
                    block * BLOCK + u % BLOCK, (1, COLS)
                )
        high, low = split(jnp.concatenate([fresh_own[1], fresh_other[1]], axis=0).T)
        fresh_values[0:HD] = high
        fresh_values[HD : 2 * HD] = low


def prepare(own_k, other_k, own_v, other_v, fresh_own, fresh_other, message):
    half = POSITIONS // 2
    source = pl.BlockSpec((1, half, HD), lambda r: (r, 0, 0))

    def whole(*shape):
        return pl.BlockSpec(shape, lambda r: (0,) * len(shape))

    return pl.pallas_call(
        prepare_kernel,
        grid=(REQS,),
        in_specs=[source] * 4 + [whole(2, TOK, HD)] * 2 + [whole(4 * PART, HEADS, HD)],
        out_specs=[
            pl.BlockSpec((1, POSITIONS, 2 * HD), lambda r: (r, 0, 0)),
            pl.BlockSpec((1, 2 * HD, POSITIONS), lambda r: (r, 0, 0)),
            whole(FRESH, 2 * HD),
            whole(2 * HD, FRESH),
            whole(FRESH, COLS),
        ],
        out_shape=[
            jax.ShapeDtypeStruct((REQS, POSITIONS, 2 * HD), jnp.bfloat16),
            jax.ShapeDtypeStruct((REQS, 2 * HD, POSITIONS), jnp.bfloat16),
            jax.ShapeDtypeStruct((FRESH, 2 * HD), jnp.bfloat16),
            jax.ShapeDtypeStruct((2 * HD, FRESH), jnp.bfloat16),
            jax.ShapeDtypeStruct((FRESH, COLS), jnp.int32),
        ],
        compiler_params=pltpu.CompilerParams(vmem_limit_bytes=16 << 20),
        cost_estimate=pl.CostEstimate(flops=10**7, bytes_accessed=16 << 20, transcendentals=0),
        name="prepare",
    )(own_k, other_k, own_v, other_v, fresh_own, fresh_other, message)


def build_lists(lengths, plan, lists, sums):
    ends = [lengths[0]]
    for req in range(1, REQS - 1):
        ends.append(ends[-1] + lengths[req])

    def request(number):
        req = jnp.int32(0)
        for end in ends:
            req = req + (number >= end).astype(jnp.int32)
        return req

    for req in range(REQS):
        sums[LAST + req] = 0
    for group, members in enumerate(GROUPS):
        first = members[0] * MEMBER_BLOCKS

        def sort_block(j, _):
            block = plan[j]
            low = request(block * BLOCK)
            high = request(block * BLOCK + BLOCK - 1)

            def append(req, _):
                count = sums[LAST + req]
                lists[req * ROOM + count] = block * NBLOCKS + j
                sums[LAST + req] = count + 1
                return 0

            append(low, 0)

            @pl.when(high > low)
            def _():
                lax.fori_loop(low + 1, high + 1, append, 0)

            return 0

        lax.fori_loop(first, first + len(members) * MEMBER_BLOCKS, sort_block, 0)
        if group < len(GROUPS) - 1:
            for req in range(REQS):
                sums[group * REQS + req] = sums[LAST + req]


def attend_kernel(group, n_out, *refs):
    first_member = GROUPS[group][0]
    n_pieces = len(REACH) - first_member
    slots = 2 * len(GROUPS[group])
    first_block = first_member * MEMBER_BLOCKS
    lengths = refs[0]
    if group == 0:
        plan, refs = refs[1], refs[2:]
    else:
        lists, sums, held, refs = refs[1], refs[2], refs[3], refs[4:]
    pieces, refs = refs[:n_pieces], refs[n_pieces:]
    fresh_keys, fresh_values, fresh_packed, keys, values = refs[:5]
    outs, refs = refs[5 : 5 + n_out], refs[5 + n_out :]
    if group == 0:
        lists, sums, refs = refs[0], refs[1], refs[2:]
    carry, refs = refs[0], refs[1:]
    (
        queries, out, weights, rows, scores_a, scores_b, new_a, new_b, peak_a, peak_b,
        tile_req, tile_first, tile_end, tile_place, tile_last,
    ) = refs

    for index, piece in enumerate(pieces):
        queries[pl.ds(index * 4 * PART, 4 * PART)] = piece[...]
    for slot in range(slots):
        out[slot, SLOT_TOK] = jnp.zeros((HEADS, HD), jnp.float32)
    if group == 0:
        build_lists(lengths, plan, lists, sums)

    lane = lax.broadcasted_iota(jnp.int32, (1, COLS), 1) // HEADS
    lanes = lax.broadcasted_iota(jnp.int32, (HEADS, HD), 1)

    def put_block(entry, begin, end, value, level):
        block = entry // NBLOCKS
        local = lax.rem(entry, NBLOCKS) - first_block
        mine = local < slots * SLOT_TOK // BLOCK
        slot = local // (SLOT_TOK // BLOCK)
        base = lax.rem(local, SLOT_TOK // BLOCK) * BLOCK
        for u in range(BLOCK):
            number = block * BLOCK + u
            good = mine & (number >= begin) & (number < end)
            where = jnp.where(good, slot, slots)
            out[where, base + u] = value(u)
            out[where, SLOT_TOK] = jnp.where(
                lanes == base + u, level(u), out[where, SLOT_TOK]
            )

    begin = jnp.int32(0)
    tiles = jnp.int32(0)
    tile_req[0] = 0
    tile_first[0] = 0
    tile_end[0] = 1
    tile_place[0] = 0
    tile_last[0] = 0
    for req in range(REQS):
        end = begin + lengths[req]
        count = sums[group * REQS + req]
        total = sums[LAST + req]
        upto = (count + TILE_BLOCKS - 1) // TILE_BLOCKS
        done = jnp.int32(0)
        if group > 0:
            before = sums[(group - 1) * REQS + req]
            done = (before + TILE_BLOCKS - 1) // TILE_BLOCKS

            def reuse(p, _, req=req, begin=begin, end=end, done=done):
                place = (p - (done - 1) * TILE_BLOCKS) * BLOCK
                put_block(
                    lists[req * ROOM + p], begin, end,
                    lambda u: held[req, 0, place + u], lambda u: held[req, 1, place + u],
                )
                return 0

            lax.fori_loop(before, jnp.minimum(count, done * TILE_BLOCKS), reuse, 0)
            carry[req] = held[req]

        def list_tile(t, _, req=req, begin=begin, end=end, tiles=tiles, done=done, total=total):
            tile_req[tiles + t - done] = req
            tile_first[tiles + t - done] = begin
            tile_end[tiles + t - done] = end
            tile_place[tiles + t - done] = req * ROOM + t * TILE_BLOCKS
            tile_last[tiles + t - done] = req * ROOM + total - 1
            return 0

        lax.fori_loop(done, upto, list_tile, 0)
        begin = end
        tiles = tiles + upto - done

    def entry(index, b):
        return lists[jnp.minimum(tile_place[index] + b, tile_last[index])]

    def load(index):
        for b in range(TILE_BLOCKS):
            local = jnp.maximum(lax.rem(entry(index, b), NBLOCKS) - first_block, 0)
            row = local // BLOCK * PART + lax.rem(local, BLOCK) * BLOCK
            for u in range(BLOCK):
                rows[pl.ds((b * BLOCK + u) * HEADS, HEADS), :] = queries[row + u]
        high, low = split(rows[...] * SCALE)
        weights[:, 0:HD] = high
        weights[:, HD : 2 * HD] = high
        weights[:, 2 * HD : 3 * HD] = low

    def score(key):
        both = lax.dot_general(
            key, weights[:, 0 : 2 * HD], NT, preferred_element_type=jnp.float32
        )
        return both + lax.dot_general(
            key[:, 0:HD], weights[:, 2 * HD : 3 * HD], NT, preferred_element_type=jnp.float32
        )

    def score_chunk(index, c, scores, peak):
        part = score(keys[tile_req[index], pl.ds(c * CHUNK, CHUNK), :])
        scores[pl.ds(c * CHUNK, CHUNK), :] = part
        top = jnp.max(part.reshape(CHUNK // 8, 8, COLS), axis=0)
        return top if peak is None else jnp.maximum(peak, top)

    def score_fresh(index, new, peak):
        part = score(fresh_keys[...])
        number = fresh_packed[...]
        latest = jnp.zeros((1, COLS), jnp.int32)
        for b in range(TILE_BLOCKS):
            latest = jnp.where(lane // BLOCK == b, entry(index, b) // NBLOCKS, latest)
        latest = latest * BLOCK + lane % BLOCK
        allowed = (number >= tile_first[index]) & (number <= latest)
        part = jnp.where(allowed, part, NEG)
        new[...] = part
        return jnp.maximum(peak, jnp.max(part.reshape(FRESH // 8, 8, COLS), axis=0))

    def weigh(part, top):
        p = jnp.exp2(part - top)
        high, low = split(p)
        return jnp.sum(p.reshape(part.shape[0] // 8, 8, COLS), axis=0), high, low

    def accumulate(value, high, low, acc):
        first = jnp.dot(value, high, preferred_element_type=jnp.float32)
        second = jnp.dot(value[0:HD], low, preferred_element_type=jnp.float32)
        both = first[0:HD] + first[HD : 2 * HD] + second
        return both if acc is None else acc + both

    def finish(index, top, mass, acc):
        total = jnp.sum(mass, axis=0, keepdims=True)
        done = (acc / total).T.reshape(TILE, HEADS, HD)
        level = jnp.broadcast_to(top + jnp.log2(total), (HD, COLS)).T.reshape(TILE, HEADS, HD)
        req = tile_req[index]
        carry[req, 0] = done
        carry[req, 1] = level
        for b in range(TILE_BLOCKS):
            put_block(
                entry(index, b), tile_first[index], tile_end[index],
                lambda u: done[b * BLOCK + u], lambda u: level[b * BLOCK + u],
            )

    def step(now, later, scores_now, new_now, peak_now, scores_later, new_later, peak_later):
        load(later)
        top = jnp.max(peak_now[...], axis=0, keepdims=True)
        mass, high, low = weigh(new_now[...], top)
        acc = accumulate(fresh_values[...], high, low, None)
        peak = None
        for c in range(CHUNKS):
            peak = score_chunk(later, c, scores_later, peak)
            more, high, low = weigh(scores_now[pl.ds(c * CHUNK, CHUNK), :], top)
            mass = mass + more
            acc = accumulate(
                values[tile_req[now], :, pl.ds(c * CHUNK, CHUNK)], high, low, acc
            )
        peak_later[...] = score_fresh(later, new_later, peak)
        finish(now, top, mass, acc)

    load(0)
    peak = None
    for c in range(CHUNKS):
        peak = score_chunk(0, c, scores_a, peak)
    peak_a[...] = score_fresh(0, new_a, peak)

    def pair(j, _):
        for this, (a, b) in enumerate(
            (
                ((scores_a, new_a, peak_a), (scores_b, new_b, peak_b)),
                ((scores_b, new_b, peak_b), (scores_a, new_a, peak_a)),
            )
        ):
            current = 2 * j + this

            @pl.when(current < tiles)
            def _():
                step(current, jnp.minimum(current + 1, tiles - 1), *a, *b)

        return 0

    lax.fori_loop(0, (tiles + 1) // 2, pair, 0)
    for index, target in enumerate(outs):
        target[...] = out[pl.ds(2 * index, 2)]


def attend(group, lengths, tables, carry, pieces, fresh, keys, values):
    n_out = len(GROUPS[group])
    tables = list(tables) + ([] if carry is None else [carry])
    n_smem = 2 if group == 0 else 3
    n_vmem = len(pieces) + 5 + (group > 0)
    hold = jax.ShapeDtypeStruct((REQS, 2, TILE, HEADS, HD), jnp.float32)
    table_out = [
        jax.ShapeDtypeStruct((REQS * ROOM,), jnp.int32),
        jax.ShapeDtypeStruct((LAST + REQS,), jnp.int32),
    ]
    slots = 2 * n_out
    tile_table = pltpu.SMEM((MAX_TILES,), jnp.int32)
    return pl.pallas_call(
        functools.partial(attend_kernel, group, n_out),
        in_specs=[SMEM] * n_smem + [VMEM] * n_vmem,
        out_specs=[VMEM] * n_out + [SMEM] * (2 * (group == 0)) + [VMEM],
        out_shape=[jax.ShapeDtypeStruct((2, SLOT_TOK + 1, HEADS, HD), jnp.float32)] * n_out
        + table_out * (group == 0)
        + [hold],
        scratch_shapes=[
            pltpu.VMEM((len(pieces) * 4 * PART, HEADS, HD), jnp.float32),
            pltpu.VMEM((slots + 1, SLOT_TOK + 1, HEADS, HD), jnp.float32),
            pltpu.VMEM((COLS, 3 * HD), jnp.bfloat16),
            pltpu.VMEM((COLS, HD), jnp.float32),
            pltpu.VMEM((POSITIONS, COLS), jnp.float32),
            pltpu.VMEM((POSITIONS, COLS), jnp.float32),
            pltpu.VMEM((FRESH, COLS), jnp.float32),
            pltpu.VMEM((FRESH, COLS), jnp.float32),
            pltpu.VMEM((8, COLS), jnp.float32),
            pltpu.VMEM((8, COLS), jnp.float32),
        ]
        + [tile_table] * 5,
        compiler_params=pltpu.CompilerParams(vmem_limit_bytes=16 << 20),
        cost_estimate=pl.CostEstimate(
            flops=n_out * 8 * 10**9, bytes_accessed=8 << 20, transcendentals=10**6
        ),
        name="attend",
    )(lengths, *tables, *pieces, *fresh, keys, values)


def blend(parts, store, store_level=None):
    levels = [part[SLOT_TOK] for part in parts]
    top = levels[0]
    for level in levels[1:]:
        top = jnp.maximum(top, level)
    shares = [jnp.exp2(level - top) for level in levels]
    total = shares[0]
    for share in shares[1:]:
        total = total + share
    shares = [share / total for share in shares]
    for t in range(SLOT_TOK):
        acc = parts[0][t] * shares[0][:, t : t + 1]
        for part, share in zip(parts[1:], shares[1:]):
            acc = acc + part[t] * share[:, t : t + 1]
        store(t, acc)
    if store_level is not None:
        store_level(top + jnp.log2(total))


def put(ref, slot, t, value):
    ref[slot, t] = value


def hop_kernel(*refs):
    n = len(refs) // 3
    for part, got, out in zip(refs[:n], refs[n : 2 * n], refs[2 * n :]):
        for slot in range(2):
            store = functools.partial(put, out, slot)
            blend((part.at[slot], got.at[slot]), store, functools.partial(store, SLOT_TOK))


def hop(parts, got):
    n = len(parts)
    return pl.pallas_call(
        hop_kernel,
        in_specs=[VMEM] * (2 * n),
        out_specs=[VMEM] * n,
        out_shape=[jax.ShapeDtypeStruct(parts[0].shape, jnp.float32)] * n,
        compiler_params=pltpu.CompilerParams(vmem_limit_bytes=4 << 20),
        name="hop",
    )(*parts, *got)


def arrive_kernel(own, up_in, down_in, keep, give):
    for slot, out in enumerate((keep, give)):
        store = functools.partial(put, out, 0)
        blend(
            (own.at[slot], up_in.at[slot], down_in.at[slot]),
            store, functools.partial(store, SLOT_TOK),
        )


def arrive(own, up_in, down_in):
    shape = (1,) + own.shape[1:]
    return pl.pallas_call(
        arrive_kernel,
        in_specs=[VMEM] * 3,
        out_specs=[VMEM] * 2,
        out_shape=[jax.ShapeDtypeStruct(shape, jnp.float32)] * 2,
        compiler_params=pltpu.CompilerParams(vmem_limit_bytes=4 << 20),
        name="arrive",
    )(own, up_in, down_in)


def settle_kernel(one, two, keep, give):
    def store(t, value):
        if t < TOK:
            keep[t] = value
        else:
            give[t - TOK] = value

    blend((one.at[0], two.at[0]), store)


def settle(one, two):
    return pl.pallas_call(
        settle_kernel,
        in_specs=[VMEM] * 2,
        out_specs=[VMEM] * 2,
        out_shape=[jax.ShapeDtypeStruct((TOK, HEADS, HD), jnp.float32)] * 2,
        compiler_params=pltpu.CompilerParams(vmem_limit_bytes=4 << 20),
        name="settle",
    )(one, two)


def body(queries, new_kv, cache_keys, cache_values, new_lengths, block_plan):
    core = lax.axis_index("ctx") % 2
    n_ctx = 32
    n_head = 8

    def send(x, target):
        return lax.ppermute(x, "ctx", [(i, target(i)) for i in range(n_ctx)])

    def across(i):
        return i ^ 1

    def beside(i):
        return i ^ 2

    def along(k):
        return lambda i: (i + 4 * k) % n_ctx

    up, down = along(1), along(-1)
    tie = lax.optimization_barrier

    q = queries.reshape(TOK, 2, HEADS, HD)
    number = jnp.pad(
        block_plan.astype(jnp.float32)[None, None], ((0, 0), (0, HEADS - 1), (0, HD - TOK // BLOCK))
    )
    mine = jnp.concatenate([lax.dynamic_index_in_dim(q, core, 1, keepdims=False), number])
    theirs = jnp.concatenate([lax.dynamic_index_in_dim(q, 1 - core, 1, keepdims=False), number])
    held = {
        0: jnp.concatenate(
            [mine, send(theirs, across), send(mine, beside), send(theirs, lambda i: i ^ 3)]
        )
    }
    other_k, other_v = send(cache_keys, across), send(cache_values, across)
    fresh = new_kv[:, :, 0]
    fresh_other = send(fresh, across)
    held[-1], held[1] = send(held[0], up), send(held[0], down)
    keys, values, *fresh = prepare(
        cache_keys[:, :, 0], other_k[:, :, 0], cache_values[:, :, 0], other_v[:, :, 0],
        fresh, fresh_other, held[0],
    )
    held[-1], fresh[2] = tie((held[-1], fresh[2]))
    for k in (1, 2):
        held[-k - 1], held[k + 1] = send(held[-k], up), send(held[k], down)
    held[4] = send(held[-3], up)
    plan = jnp.concatenate(
        [held[k].reshape(4, PART, HEADS, HD)[:, TOK, 0, : TOK // BLOCK] for k in REACH]
    )
    plan = plan.reshape(NBLOCKS).astype(jnp.int32)

    def call(group, tables, carry):
        pieces = [held[k] for k in REACH[GROUPS[group][0] :]]
        return attend(group, new_lengths, tables, carry, pieces, fresh, keys, values)

    part, *tables, carry = call(0, (plan,), None)
    carry, part = tie((carry, part))
    got = (send(part, up),)
    for group in range(1, 4):
        up_part, down_part, carry = call(group, tables, carry)
        if group == 1:
            sent = (*hop((up_part,), got), down_part)
        else:
            sent = hop((up_part, down_part), got)
        carry, *sent = tie((carry, *sent))
        got = (send(sent[0], up), send(sent[1], down))
    up_in, down_in = got
    own, _ = call(4, tables, carry)
    keep, give = arrive(own, up_in, down_in)
    keep, give = settle(keep, send(give, beside))
    got = send(give, across)
    first = jnp.where(core == 0, keep, got)
    second = jnp.where(core == 0, got, keep)
    wide = jnp.concatenate([first, second], axis=1).reshape(n_head, TOK // n_head, 1, 2 * HEADS * HD)
    regrouped = lax.all_to_all(wide, "head", split_axis=0, concat_axis=2, tiled=True)
    return regrouped.reshape(TOK // n_head, n_head * 2 * HEADS * HD)


def solution(mesh):
    placed = (
        P("ctx", "head", None),
        P(None, "ctx", "head", None),
        P(None, "ctx", "head", None),
        P(None, "ctx", "head", None),
        P(),
        P("ctx"),
    )
    return jax.shard_map(
        body, mesh=mesh, in_specs=placed, out_specs=P(("ctx", "head"), None), check_vma=False
    )
```

```python
import functools
import math

import jax
import jax.numpy as jnp
from jax import lax
from jax.experimental import pallas as pl
from jax.experimental.pallas import tpu as pltpu
from jax.sharding import PartitionSpec as P

REQS = 4
HD = 128
HEADS = 8
TOK = 16
BLOCK = 4
TILE = 32
COLS = TILE * HEADS
POSITIONS = 2048
HALF = POSITIONS // 2
CHUNK = 512
CHUNKS = POSITIONS // CHUNK
HALF_CHUNKS = CHUNKS // 2
FRESH = 2 * TOK
SLOT_TOK = 2 * TOK
PART = TOK + 1
MEMBER_BLOCKS = 4 * TOK // BLOCK
NBLOCKS = 8 * MEMBER_BLOCKS
TILE_BLOCKS = TILE // BLOCK
MAX_TILES = 12
REACH = (4, 3, -3, 2, -2, 1, -1, 0)
GROUPS = ((0,), (1, 2), (3, 4), (5, 6), (7,))
ROOM = 64
LAST = (len(GROUPS) - 1) * REQS
SUMS = REQS * ROOM
LENGTHS = SUMS + LAST + REQS
VMEM = pl.BlockSpec(memory_space=pltpu.VMEM)
SMEM = pl.BlockSpec(memory_space=pltpu.SMEM)
NEG = -1e30
SCALE = HD ** (-0.5) * math.log2(math.e)
NT = (((1,), (1,)), ((), ()))


def split(x):
    high = x.astype(jnp.bfloat16)
    low = (x - high.astype(jnp.float32)).astype(jnp.bfloat16)
    return high, low


def prepare_kernel(k, v, *refs):
    keys, values = refs[-2:] if len(refs) == 2 else refs[3:5]
    high, low = split(k[0])
    keys[0, :, 0:HD] = high
    keys[0, :, HD : 2 * HD] = low
    high, low = split(v[0].T)
    values[0, 0:HD] = high
    values[0, HD : 2 * HD] = low
    if len(refs) == 2:
        return
    fresh_own, fresh_other, message = refs[:3]
    fresh_keys, fresh_values, fresh_packed = refs[5:]

    @pl.when(pl.program_id(0) == 0)
    def _():
        for half, fresh in enumerate((fresh_own, fresh_other)):
            span = pl.ds(half * TOK, TOK)
            high, low = split(fresh[0])
            fresh_keys[span, 0:HD] = high
            fresh_keys[span, HD : 2 * HD] = low
            plan = message[half * PART + TOK].astype(jnp.int32)
            for u in range(TOK):
                block = plan[0:1, u // BLOCK : u // BLOCK + 1]
                fresh_packed[half * TOK + u : half * TOK + u + 1, :] = jnp.broadcast_to(
                    block * BLOCK + u % BLOCK, (1, COLS)
                )
        high, low = split(jnp.concatenate([fresh_own[1], fresh_other[1]], axis=0).T)
        fresh_values[0:HD] = high
        fresh_values[HD : 2 * HD] = low


def prepare(k, v, *fresh):
    def whole(*shape):
        return pl.BlockSpec(shape, lambda r: (0,) * len(shape))

    source = pl.BlockSpec((1, HALF, HD), lambda r: (r, 0, 0))
    shapes = [(REQS, HALF, 2 * HD), (REQS, 2 * HD, HALF)]
    blocks = [pl.BlockSpec((1,) + shape[1:], lambda r: (r, 0, 0)) for shape in shapes]
    kinds = [jnp.bfloat16] * 2
    if fresh:
        extra = [(FRESH, 2 * HD), (2 * HD, FRESH), (FRESH, COLS)]
        shapes += extra
        blocks += [whole(*shape) for shape in extra]
        kinds += [jnp.bfloat16, jnp.bfloat16, jnp.int32]
    return pl.pallas_call(
        prepare_kernel,
        grid=(REQS,),
        in_specs=[source] * 2 + [whole(*x.shape) for x in fresh],
        out_specs=blocks,
        out_shape=[jax.ShapeDtypeStruct(*pair) for pair in zip(shapes, kinds)],
        compiler_params=pltpu.CompilerParams(vmem_limit_bytes=8 << 20),
        cost_estimate=pl.CostEstimate(flops=10**7, bytes_accessed=8 << 20, transcendentals=0),
        name="prepare",
    )(k, v, *fresh)


def build_lists(lengths, plan, table):
    bounds = [jnp.int32(0)]
    for req in range(REQS):
        table[LENGTHS + req] = lengths[req]
        bounds.append(bounds[-1] + lengths[req])
    counts = (jnp.int32(0),) * REQS
    for group, members in enumerate(GROUPS):
        first = members[0] * MEMBER_BLOCKS

        def sort_block(j, counts):
            block = plan[j // BLOCK, lax.rem(j, BLOCK)]
            value = block * NBLOCKS + j
            low = block * BLOCK
            new = []
            for req in range(REQS):
                table[req * ROOM + counts[req]] = value
                inside = (low + BLOCK > bounds[req]) & (low < bounds[req + 1])
                new.append(counts[req] + inside.astype(jnp.int32))
            return tuple(new)

        counts = lax.fori_loop(
            first, first + len(members) * MEMBER_BLOCKS, sort_block, counts, unroll=4
        )
        for req in range(REQS):
            table[SUMS + group * REQS + req] = counts[req]


def attend_kernel(group, n_out, *refs):
    first_member = GROUPS[group][0]
    n_pieces = len(REACH) - first_member
    slots = 2 * len(GROUPS[group])
    first_block = first_member * MEMBER_BLOCKS
    if group == 0:
        lengths, refs = refs[0], refs[1:]
    else:
        table, held, refs = refs[0], refs[1], refs[2:]
    pieces, refs = refs[:n_pieces], refs[n_pieces:]
    fresh_keys, fresh_values, fresh_packed = refs[:3]
    keys, values, refs = refs[3:5], refs[5:7], refs[7:]
    outs, refs = refs[:n_out], refs[n_out:]
    if group == 0:
        table, refs = refs[0], refs[1:]
        numbers, plan, sem = refs[-3:]
        refs = refs[:-3]
    carry, refs = refs[0], refs[1:]
    (
        queries, out, weights_a, weights_b, rows, scores_a, scores_b, new_a, new_b,
        peak_a, peak_b, ready, ready_level,
        tile_req, tile_first, tile_end, tile_place, tile_last,
    ) = refs

    if group == 0:
        for index, piece in enumerate(pieces):
            for part in range(4):
                row = 4 * index + part
                numbers[row : row + 1] = piece[part * PART + TOK, 0:1].astype(jnp.int32)
        copy = pltpu.make_async_copy(numbers, plan, sem)
        copy.start()
    for index, piece in enumerate(pieces):
        queries[pl.ds(index * 4 * PART, 4 * PART)] = piece[...]
    for slot in range(slots):
        out[slot, SLOT_TOK] = jnp.zeros((HEADS, HD), jnp.float32)
    if group == 0:
        copy.wait()
        build_lists(lengths, plan, table)

    lane = lax.broadcasted_iota(jnp.int32, (1, COLS), 1) // HEADS
    lanes = lax.broadcasted_iota(jnp.int32, (HEADS, HD), 1)

    def put_block(entry, begin, end, value, level):
        block = entry // NBLOCKS
        local = lax.rem(entry, NBLOCKS) - first_block
        mine = local < slots * SLOT_TOK // BLOCK
        slot = local // (SLOT_TOK // BLOCK)
        base = lax.rem(local, SLOT_TOK // BLOCK) * BLOCK
        for u in range(BLOCK):
            number = block * BLOCK + u
            good = mine & (number >= begin) & (number < end)
            where = jnp.where(good, slot, slots)
            out[where, base + u] = value(u)
            out[where, SLOT_TOK] = jnp.where(
                lanes == base + u, level(u), out[where, SLOT_TOK]
            )

    begin = jnp.int32(0)
    tiles = jnp.int32(0)
    tile_req[0] = 0
    tile_first[0] = 0
    tile_end[0] = 1
    tile_place[0] = 0
    tile_last[0] = 0
    for req in range(REQS):
        end = begin + table[LENGTHS + req]
        count = table[SUMS + group * REQS + req]
        total = table[SUMS + LAST + req]
        upto = (count + TILE_BLOCKS - 1) // TILE_BLOCKS
        done = jnp.int32(0)
        if group > 0:
            before = table[SUMS + (group - 1) * REQS + req]
            done = (before + TILE_BLOCKS - 1) // TILE_BLOCKS

            def reuse(p, _, req=req, begin=begin, end=end, done=done):
                place = (p - (done - 1) * TILE_BLOCKS) * BLOCK
                put_block(
                    table[req * ROOM + p], begin, end,
                    lambda u: held[req, 0, place + u], lambda u: held[req, 1, place + u],
                )
                return 0

            lax.fori_loop(before, jnp.minimum(count, done * TILE_BLOCKS), reuse, 0)
            carry[req] = held[req]

        def list_tile(t, _, req=req, begin=begin, end=end, tiles=tiles, done=done, total=total):
            tile_req[tiles + t - done] = req
            tile_first[tiles + t - done] = begin
            tile_end[tiles + t - done] = end
            tile_place[tiles + t - done] = req * ROOM + t * TILE_BLOCKS
            tile_last[tiles + t - done] = req * ROOM + total - 1
            return 0

        lax.fori_loop(done, upto, list_tile, 0)
        begin = end
        tiles = tiles + upto - done

    def entry(index, b):
        return table[jnp.minimum(tile_place[index] + b, tile_last[index])]

    def load(index, weights):
        for b in range(TILE_BLOCKS):
            local = jnp.maximum(lax.rem(entry(index, b), NBLOCKS) - first_block, 0)
            row = local // BLOCK * PART + lax.rem(local, BLOCK) * BLOCK
            for u in range(BLOCK):
                rows[pl.ds((b * BLOCK + u) * HEADS, HEADS), :] = queries[row + u]
        high, low = split(rows[...] * SCALE)
        weights[:, 0:HD] = high
        weights[:, HD : 2 * HD] = high
        weights[:, 2 * HD : 3 * HD] = low

    def score(key, weights):
        both = lax.dot_general(
            key, weights[:, 0 : 2 * HD], NT, preferred_element_type=jnp.float32
        )
        return both + lax.dot_general(
            key[:, 0:HD], weights[:, 2 * HD : 3 * HD], NT, preferred_element_type=jnp.float32
        )

    def score_chunk(index, c, weights, scores, peak):
        part = score(
            keys[c // HALF_CHUNKS][tile_req[index], pl.ds(c % HALF_CHUNKS * CHUNK, CHUNK), :],
            weights,
        )
        scores[pl.ds(c * CHUNK, CHUNK), :] = part
        top = jnp.max(part.reshape(CHUNK // 8, 8, COLS), axis=0)
        return top if peak is None else jnp.maximum(peak, top)

    def score_fresh(index, weights, new, peak):
        part = score(fresh_keys[...], weights)
        number = fresh_packed[...]
        latest = jnp.zeros((1, COLS), jnp.int32)
        for b in range(TILE_BLOCKS):
            latest = jnp.where(lane // BLOCK == b, entry(index, b) // NBLOCKS, latest)
        latest = latest * BLOCK + lane % BLOCK
        allowed = (number >= tile_first[index]) & (number <= latest)
        part = jnp.where(allowed, part, NEG)
        new[...] = part
        return jnp.maximum(peak, jnp.max(part.reshape(FRESH // 8, 8, COLS), axis=0))

    def weigh(part, top):
        p = jnp.exp2(part - top)
        high, low = split(p)
        return jnp.sum(p.reshape(part.shape[0] // 8, 8, COLS), axis=0), high, low

    def accumulate(value, high, low, acc):
        first = jnp.dot(value, high, preferred_element_type=jnp.float32)
        second = jnp.dot(value[0:HD], low, preferred_element_type=jnp.float32)
        both = first[0:HD] + first[HD : 2 * HD] + second
        return both if acc is None else acc + both

    def finish(index):
        done = ready[...].T.reshape(TILE, HEADS, HD)
        level = jnp.broadcast_to(ready_level[0:1], (HD, COLS)).T.reshape(TILE, HEADS, HD)
        req = tile_req[index]
        carry[req, 0] = done
        carry[req, 1] = level
        for b in range(TILE_BLOCKS):
            put_block(
                entry(index, b), tile_first[index], tile_end[index],
                lambda u: done[b * BLOCK + u], lambda u: level[b * BLOCK + u],
            )

    def step(now, follow, mine, other):
        weights_now, scores_now, new_now, peak_now = mine
        weights_later, scores_later, new_later, peak_later = other
        finish(jnp.maximum(now - 1, 0))
        later = now + 1
        top = jnp.max(peak_now[...], axis=0, keepdims=True)
        mass, high, low = weigh(new_now[...], top)
        acc = accumulate(fresh_values[...], high, low, None)
        peak = None
        for c in range(CHUNKS):
            if follow:
                peak = score_chunk(later, c, weights_later, scores_later, peak)
            more, high, low = weigh(scores_now[pl.ds(c * CHUNK, CHUNK), :], top)
            mass = mass + more
            acc = accumulate(
                values[c // HALF_CHUNKS][tile_req[now], :, pl.ds(c % HALF_CHUNKS * CHUNK, CHUNK)],
                high, low, acc,
            )
        if follow:
            peak_later[...] = score_fresh(later, weights_later, new_later, peak)
            load(jnp.minimum(now + 2, tiles - 1), weights_now)
        total = jnp.sum(mass, axis=0, keepdims=True)
        ready[...] = acc / total
        ready_level[0:1] = top + jnp.log2(total)

    even = (weights_a, scores_a, new_a, peak_a)
    odd = (weights_b, scores_b, new_b, peak_b)
    ready[...] = jnp.zeros_like(ready)
    ready_level[...] = jnp.zeros_like(ready_level)
    load(0, weights_a)
    load(jnp.clip(tiles - 1, 0, 1), weights_b)
    peak = None
    for c in range(CHUNKS):
        peak = score_chunk(0, c, weights_a, scores_a, peak)
    peak_a[...] = score_fresh(0, weights_a, new_a, peak)

    def pair(j, _):
        for this, (a, b) in enumerate(((even, odd), (odd, even))):
            current = 2 * j + this

            @pl.when(current < tiles - 1)
            def _():
                step(current, True, a, b)

            @pl.when(current == tiles - 1)
            def _():
                step(current, False, a, b)

        return 0

    lax.fori_loop(0, (tiles + 1) // 2, pair, 0)

    @pl.when(tiles > 0)
    def _():
        finish(tiles - 1)

    for index, target in enumerate(outs):
        target[...] = out[pl.ds(2 * index, 2)]


def attend(group, table, carry, pieces, fresh, keys, values):
    n_out = len(GROUPS[group])
    carried = [] if carry is None else [carry]
    n_vmem = len(pieces) + 7 + len(carried)
    hold = jax.ShapeDtypeStruct((REQS, 2, TILE, HEADS, HD), jnp.float32)
    table_out = [jax.ShapeDtypeStruct((LENGTHS + REQS,), jnp.int32)]
    slots = 2 * n_out
    tile_table = pltpu.SMEM((MAX_TILES,), jnp.int32)
    return pl.pallas_call(
        functools.partial(attend_kernel, group, n_out),
        in_specs=[SMEM] + [VMEM] * n_vmem,
        out_specs=[VMEM] * n_out + [SMEM] * (group == 0) + [VMEM],
        out_shape=[jax.ShapeDtypeStruct((2, SLOT_TOK + 1, HEADS, HD), jnp.float32)] * n_out
        + table_out * (group == 0)
        + [hold],
        scratch_shapes=[
            pltpu.VMEM((len(pieces) * 4 * PART, HEADS, HD), jnp.float32),
            pltpu.VMEM((slots + 1, SLOT_TOK + 1, HEADS, HD), jnp.float32),
            pltpu.VMEM((COLS, 3 * HD), jnp.bfloat16),
            pltpu.VMEM((COLS, 3 * HD), jnp.bfloat16),
            pltpu.VMEM((COLS, HD), jnp.float32),
            pltpu.VMEM((POSITIONS, COLS), jnp.float32),
            pltpu.VMEM((POSITIONS, COLS), jnp.float32),
            pltpu.VMEM((FRESH, COLS), jnp.float32),
            pltpu.VMEM((FRESH, COLS), jnp.float32),
            pltpu.VMEM((8, COLS), jnp.float32),
            pltpu.VMEM((8, COLS), jnp.float32),
            pltpu.VMEM((HD, COLS), jnp.float32),
            pltpu.VMEM((8, COLS), jnp.float32),
        ]
        + [tile_table] * 5
        + [
            pltpu.VMEM((4 * len(REACH), HD), jnp.int32),
            pltpu.SMEM((4 * len(REACH), HD), jnp.int32),
            pltpu.SemaphoreType.DMA,
        ]
        * (group == 0),
        compiler_params=pltpu.CompilerParams(vmem_limit_bytes=16 << 20),
        cost_estimate=pl.CostEstimate(
            flops=n_out * 8 * 10**9, bytes_accessed=8 << 20, transcendentals=10**6
        ),
        name="attend",
    )(table, *carried, *pieces, *fresh, *keys, *values)


def blend(parts, store, store_level=None):
    levels = [part[SLOT_TOK] for part in parts]
    top = levels[0]
    for level in levels[1:]:
        top = jnp.maximum(top, level)
    shares = [jnp.exp2(level - top) for level in levels]
    total = shares[0]
    for share in shares[1:]:
        total = total + share
    shares = [share / total for share in shares]
    for t in range(SLOT_TOK):
        acc = parts[0][t] * shares[0][:, t : t + 1]
        for part, share in zip(parts[1:], shares[1:]):
            acc = acc + part[t] * share[:, t : t + 1]
        store(t, acc)
    if store_level is not None:
        store_level(top + jnp.log2(total))


def put(ref, slot, t, value):
    ref[slot, t] = value


def hop_kernel(*refs):
    n = len(refs) // 3
    for part, got, out in zip(refs[:n], refs[n : 2 * n], refs[2 * n :]):
        for slot in range(2):
            store = functools.partial(put, out, slot)
            blend((part.at[slot], got.at[slot]), store, functools.partial(store, SLOT_TOK))


def hop(parts, got):
    n = len(parts)
    return pl.pallas_call(
        hop_kernel,
        in_specs=[VMEM] * (2 * n),
        out_specs=[VMEM] * n,
        out_shape=[jax.ShapeDtypeStruct(parts[0].shape, jnp.float32)] * n,
        compiler_params=pltpu.CompilerParams(vmem_limit_bytes=4 << 20),
        name="hop",
    )(*parts, *got)


def arrive_kernel(corner, own, up_in, down_in, out):
    pair = TOK // HEADS
    for slot in range(2):
        def store(t, value, slot=slot):
            target = jnp.bitwise_xor(corner[0], 2 * slot + t // TOK)
            inside = t % TOK
            out[target, inside // pair, inside % pair] = value

        def store_level(level, slot=slot):
            for half in range(2):
                target = jnp.bitwise_xor(corner[0], 2 * slot + half)
                for h in range(HEADS):
                    first = half * TOK + h * pair
                    out[target, h, pair] = jnp.concatenate(
                        [level[:, first : first + pair], jnp.zeros((HEADS, HD - pair), jnp.float32)],
                        axis=1,
                    )

        blend((own.at[slot], up_in.at[slot], down_in.at[slot]), store, store_level)


def arrive(corner, own, up_in, down_in):
    return pl.pallas_call(
        arrive_kernel,
        in_specs=[SMEM] + [VMEM] * 3,
        out_specs=VMEM,
        out_shape=jax.ShapeDtypeStruct((4, HEADS, TOK // HEADS + 1, HEADS, HD), jnp.float32),
        compiler_params=pltpu.CompilerParams(vmem_limit_bytes=4 << 20),
        name="arrive",
    )(corner, own, up_in, down_in)


def settle_kernel(parts, out):
    pair = TOK // HEADS
    for core in range(2):
        for h in range(HEADS):
            one, two = parts.at[core, h], parts.at[2 + core, h]
            levels = (one[pair], two[pair])
            top = jnp.maximum(*levels)
            shares = [jnp.exp2(level - top) for level in levels]
            total = shares[0] + shares[1]
            for t in range(pair):
                value = one[t] * (shares[0] / total)[:, t : t + 1]
                value = value + two[t] * (shares[1] / total)[:, t : t + 1]
                out[t, pl.ds((2 * h + core) * HEADS, HEADS), :] = value


def settle(parts):
    return pl.pallas_call(
        settle_kernel,
        in_specs=[VMEM],
        out_specs=VMEM,
        out_shape=jax.ShapeDtypeStruct((TOK // HEADS, 2 * HEADS * HEADS, HD), jnp.float32),
        compiler_params=pltpu.CompilerParams(vmem_limit_bytes=4 << 20),
        name="settle",
    )(parts)


def pack_kernel(core, plan, queries, mine, theirs):
    for out, half in ((mine, core[0]), (theirs, 1 - core[0])):
        out[0:TOK] = queries[:, pl.ds(pl.multiple_of(half * HEADS, HEADS), HEADS), :]
        lanes = lax.broadcasted_iota(jnp.int32, (HEADS, HD), 1)
        number = jnp.zeros((HEADS, HD), jnp.int32)
        for b in range(TOK // BLOCK):
            number = jnp.where(lanes == b, plan[b], number)
        out[TOK] = number.astype(jnp.float32)


def pack(core, plan, queries):
    return pl.pallas_call(
        pack_kernel,
        in_specs=[SMEM, SMEM, VMEM],
        out_specs=[VMEM] * 2,
        out_shape=[jax.ShapeDtypeStruct((PART, HEADS, HD), jnp.float32)] * 2,
        compiler_params=pltpu.CompilerParams(vmem_limit_bytes=2 << 20),
        name="pack",
    )(core, plan, queries)


def body(queries, new_kv, cache_keys, cache_values, new_lengths, block_plan):
    me = lax.axis_index("ctx")
    core = me % 2
    corner = (me % 4).reshape(1)
    n_ctx = 32
    n_head = 8

    def send(x, target):
        return lax.ppermute(x, "ctx", [(i, target(i)) for i in range(n_ctx)])

    def across(i):
        return i ^ 1

    def beside(i):
        return i ^ 2

    def along(k):
        return lambda i: (i + 4 * k) % n_ctx

    up, down = along(1), along(-1)
    tie = lax.optimization_barrier

    mine, theirs = pack(core.reshape(1), block_plan, queries.reshape(TOK, 2 * HEADS, HD))
    held = {
        0: jnp.concatenate(
            [mine, send(theirs, across), send(mine, beside), send(theirs, lambda i: i ^ 3)]
        )
    }
    corner, held[0], cache_keys, cache_values = tie((corner, held[0], cache_keys, cache_values))
    held[-1], held[1] = send(held[0], up), send(held[0], down)
    other_k, other_v = send(cache_keys, across), send(cache_values, across)
    fresh = new_kv[:, :, 0]
    fresh_other = send(fresh, across)
    own_half = list(prepare(cache_keys[:, :, 0], cache_values[:, :, 0]))
    held[-1], own_half[0] = tie((held[-1], own_half[0]))
    held[-2], held[2] = send(held[-1], up), send(held[1], down)
    *other_half, fresh_keys, fresh_values, fresh_packed = prepare(
        other_k[:, :, 0], other_v[:, :, 0], fresh, fresh_other, held[0]
    )
    fresh = (fresh_keys, fresh_values, fresh_packed)
    held[-2], other_half[0] = tie((held[-2], other_half[0]))
    held[-3], held[3] = send(held[-2], up), send(held[2], down)
    held[4] = send(held[-3], up)
    keys, values = zip(own_half, other_half)

    def call(group, table, carry):
        pieces = [held[k] for k in REACH[GROUPS[group][0] :]]
        return attend(group, table, carry, pieces, fresh, keys, values)

    part, table, carry = call(0, new_lengths, None)
    carry, part = tie((carry, part))
    got = (send(part, up),)
    for group in range(1, 4):
        up_part, down_part, carry = call(group, table, carry)
        if group == 1:
            sent = (*hop((up_part,), got), down_part)
        else:
            sent = hop((up_part, down_part), got)
        carry, *sent = tie((carry, *sent))
        got = (send(sent[0], up), send(sent[1], down))
    own, _ = call(4, table, carry)
    parts = arrive(corner, own, *got)
    plane = 4 * n_head
    home = lax.all_to_all(
        parts.reshape((plane,) + parts.shape[2:]), ("ctx", "head"),
        split_axis=0, concat_axis=0, tiled=True,
        axis_index_groups=[[z * plane + i for i in range(plane)] for z in range(n_ctx // 4)],
    )
    return settle(home.reshape(parts.shape)).reshape(TOK // n_head, n_head * 2 * HEADS * HD)


def solution(mesh):
    placed = (
        P("ctx", "head", None),
        P(None, "ctx", "head", None),
        P(None, "ctx", "head", None),
        P(None, "ctx", "head", None),
        P(),
        P("ctx"),
    )
    return jax.shard_map(
        body, mesh=mesh, in_specs=placed, out_specs=P(("ctx", "head"), None), check_vma=False
    )
```

```python
import functools
import math

import jax
import jax.numpy as jnp
from jax import lax
from jax.experimental import pallas as pl
from jax.experimental.pallas import tpu as pltpu
from jax.sharding import PartitionSpec as P

REQS = 4
HD = 128
HEADS = 8
TOK = 16
BLOCK = 4
TILE = 32
COLS = TILE * HEADS
POSITIONS = 2048
HALF = POSITIONS // 2
CHUNK = 512
CHUNKS = POSITIONS // CHUNK
HALF_CHUNKS = CHUNKS // 2
FRESH = 2 * TOK
SLOT_TOK = 2 * TOK
PART = TOK + 1
MEMBER_BLOCKS = 4 * TOK // BLOCK
NBLOCKS = 8 * MEMBER_BLOCKS
TILE_BLOCKS = TILE // BLOCK
MAX_TILES = 12
REACH = (4, 3, -3, 2, -2, 1, -1, 0)
GROUPS = ((0,), (1, 2), (3, 4), (5, 6), (7,))
ROOM = 64
LAST = (len(GROUPS) - 1) * REQS
SUMS = REQS * ROOM
LENGTHS = SUMS + LAST + REQS
VMEM = pl.BlockSpec(memory_space=pltpu.VMEM)
SMEM = pl.BlockSpec(memory_space=pltpu.SMEM)
NEG = -1e30
SCALE = HD ** (-0.5) * math.log2(math.e)
NT = (((1,), (1,)), ((), ()))


def split(x):
    high = x.astype(jnp.bfloat16)
    low = (x - high.astype(jnp.float32)).astype(jnp.bfloat16)
    return high, low


def prepare_kernel(k, v, *refs):
    keys, values = refs[-2:] if len(refs) == 2 else refs[3:5]
    high, low = split(k[0])
    keys[0, :, 0:HD] = high
    keys[0, :, HD : 2 * HD] = low
    high, low = split(v[0].T)
    values[0, 0:HD] = high
    values[0, HD : 2 * HD] = low
    if len(refs) == 2:
        return
    fresh_own, fresh_other, message = refs[:3]
    fresh_keys, fresh_values, fresh_packed = refs[5:]

    @pl.when(pl.program_id(0) == 0)
    def _():
        for half, fresh in enumerate((fresh_own, fresh_other)):
            span = pl.ds(half * TOK, TOK)
            high, low = split(fresh[0])
            fresh_keys[span, 0:HD] = high
            fresh_keys[span, HD : 2 * HD] = low
            plan = message[half * PART + TOK].astype(jnp.int32)
            for u in range(TOK):
                block = plan[0:1, u // BLOCK : u // BLOCK + 1]
                fresh_packed[half * TOK + u : half * TOK + u + 1, :] = jnp.broadcast_to(
                    block * BLOCK + u % BLOCK, (1, COLS)
                )
        high, low = split(jnp.concatenate([fresh_own[1], fresh_other[1]], axis=0).T)
        fresh_values[0:HD] = high
        fresh_values[HD : 2 * HD] = low


def prepare(k, v, *fresh):
    def whole(*shape):
        return pl.BlockSpec(shape, lambda r: (0,) * len(shape))

    source = pl.BlockSpec((1, HALF, HD), lambda r: (r, 0, 0))
    shapes = [(REQS, HALF, 2 * HD), (REQS, 2 * HD, HALF)]
    blocks = [pl.BlockSpec((1,) + shape[1:], lambda r: (r, 0, 0)) for shape in shapes]
    kinds = [jnp.bfloat16] * 2
    if fresh:
        extra = [(FRESH, 2 * HD), (2 * HD, FRESH), (FRESH, COLS)]
        shapes += extra
        blocks += [whole(*shape) for shape in extra]
        kinds += [jnp.bfloat16, jnp.bfloat16, jnp.int32]
    return pl.pallas_call(
        prepare_kernel,
        grid=(REQS,),
        in_specs=[source] * 2 + [whole(*x.shape) for x in fresh],
        out_specs=blocks,
        out_shape=[jax.ShapeDtypeStruct(*pair) for pair in zip(shapes, kinds)],
        compiler_params=pltpu.CompilerParams(vmem_limit_bytes=8 << 20),
        cost_estimate=pl.CostEstimate(flops=10**7, bytes_accessed=8 << 20, transcendentals=0),
        name="prepare",
    )(k, v, *fresh)


def build_lists(lengths, plan, table):
    bounds = [jnp.int32(0)]
    for req in range(REQS):
        table[LENGTHS + req] = lengths[req]
        bounds.append(bounds[-1] + lengths[req])
    counts = (jnp.int32(0),) * REQS
    for group, members in enumerate(GROUPS):
        first = members[0] * MEMBER_BLOCKS

        def sort_block(j, counts):
            block = plan[j // BLOCK, lax.rem(j, BLOCK)]
            value = block * NBLOCKS + j
            low = block * BLOCK
            new = []
            for req in range(REQS):
                table[req * ROOM + counts[req]] = value
                inside = (low + BLOCK > bounds[req]) & (low < bounds[req + 1])
                new.append(counts[req] + inside.astype(jnp.int32))
            return tuple(new)

        counts = lax.fori_loop(
            first, first + len(members) * MEMBER_BLOCKS, sort_block, counts, unroll=4
        )
        for req in range(REQS):
            table[SUMS + group * REQS + req] = counts[req]


def attend_kernel(group, n_out, *refs):
    first_member = GROUPS[group][0]
    n_pieces = 2 * (len(REACH) - first_member)
    slots = 2 * len(GROUPS[group])
    first_block = first_member * MEMBER_BLOCKS
    if group == 0:
        lengths, refs = refs[0], refs[1:]
    else:
        table, held, refs = refs[0], refs[1], refs[2:]
    pieces, refs = refs[:n_pieces], refs[n_pieces:]
    fresh_keys, fresh_values, fresh_packed = refs[:3]
    keys, values, refs = refs[3:5], refs[5:7], refs[7:]
    outs, refs = refs[:n_out], refs[n_out:]
    if group == 0:
        table, refs = refs[0], refs[1:]
        numbers, plan, sem = refs[-3:]
        refs = refs[:-3]
    carry, refs = refs[0], refs[1:]
    (
        queries, out, weights_a, weights_b, rows, scores_a, scores_b, new_a, new_b,
        peak_a, peak_b, ready, ready_level,
        tile_req, tile_first, tile_end, tile_place, tile_last,
    ) = refs

    if group == 0:
        for index, piece in enumerate(pieces):
            for part in range(2):
                row = 2 * index + part
                numbers[row : row + 1] = piece[part * PART + TOK, 0:1].astype(jnp.int32)
        copy = pltpu.make_async_copy(numbers, plan, sem)
        copy.start()
    for index, piece in enumerate(pieces):
        queries[pl.ds(index * 2 * PART, 2 * PART)] = piece[...]
    for slot in range(slots):
        out[slot, SLOT_TOK] = jnp.zeros((HEADS, HD), jnp.float32)
    if group == 0:
        copy.wait()
        build_lists(lengths, plan, table)

    lane = lax.broadcasted_iota(jnp.int32, (1, COLS), 1) // HEADS
    lanes = lax.broadcasted_iota(jnp.int32, (HEADS, HD), 1)

    def put_block(entry, begin, end, value, level):
        block = entry // NBLOCKS
        local = lax.rem(entry, NBLOCKS) - first_block
        mine = local < slots * SLOT_TOK // BLOCK
        slot = local // (SLOT_TOK // BLOCK)
        base = lax.rem(local, SLOT_TOK // BLOCK) * BLOCK
        for u in range(BLOCK):
            number = block * BLOCK + u
            good = mine & (number >= begin) & (number < end)
            where = jnp.where(good, slot, slots)
            out[where, base + u] = value(u)
            out[where, SLOT_TOK] = jnp.where(
                lanes == base + u, level(u), out[where, SLOT_TOK]
            )

    begin = jnp.int32(0)
    tiles = jnp.int32(0)
    tile_req[0] = 0
    tile_first[0] = 0
    tile_end[0] = 1
    tile_place[0] = 0
    tile_last[0] = 0
    for req in range(REQS):
        end = begin + table[LENGTHS + req]
        count = table[SUMS + group * REQS + req]
        total = table[SUMS + LAST + req]
        upto = (count + TILE_BLOCKS - 1) // TILE_BLOCKS
        done = jnp.int32(0)
        if group > 0:
            before = table[SUMS + (group - 1) * REQS + req]
            done = (before + TILE_BLOCKS - 1) // TILE_BLOCKS

            def reuse(p, _, req=req, begin=begin, end=end, done=done):
                place = (p - (done - 1) * TILE_BLOCKS) * BLOCK
                put_block(
                    table[req * ROOM + p], begin, end,
                    lambda u: held[req, 0, place + u], lambda u: held[req, 1, place + u],
                )
                return 0

            lax.fori_loop(before, jnp.minimum(count, done * TILE_BLOCKS), reuse, 0)
            carry[req] = held[req]

        def list_tile(t, _, req=req, begin=begin, end=end, tiles=tiles, done=done, total=total):
            tile_req[tiles + t - done] = req
            tile_first[tiles + t - done] = begin
            tile_end[tiles + t - done] = end
            tile_place[tiles + t - done] = req * ROOM + t * TILE_BLOCKS
            tile_last[tiles + t - done] = req * ROOM + total - 1
            return 0

        lax.fori_loop(done, upto, list_tile, 0)
        begin = end
        tiles = tiles + upto - done

    def entry(index, b):
        return table[jnp.minimum(tile_place[index] + b, tile_last[index])]

    def load(index, weights):
        for b in range(TILE_BLOCKS):
            local = jnp.maximum(lax.rem(entry(index, b), NBLOCKS) - first_block, 0)
            row = local // BLOCK * PART + lax.rem(local, BLOCK) * BLOCK
            for u in range(BLOCK):
                rows[pl.ds((b * BLOCK + u) * HEADS, HEADS), :] = queries[row + u]
        high, low = split(rows[...] * SCALE)
        weights[:, 0:HD] = high
        weights[:, HD : 2 * HD] = high
        weights[:, 2 * HD : 3 * HD] = low

    def score(key, weights):
        both = lax.dot_general(
            key, weights[:, 0 : 2 * HD], NT, preferred_element_type=jnp.float32
        )
        return both + lax.dot_general(
            key[:, 0:HD], weights[:, 2 * HD : 3 * HD], NT, preferred_element_type=jnp.float32
        )

    def score_chunk(index, c, weights, scores, peak):
        part = score(
            keys[c // HALF_CHUNKS][tile_req[index], pl.ds(c % HALF_CHUNKS * CHUNK, CHUNK), :],
            weights,
        )
        scores[pl.ds(c * CHUNK, CHUNK), :] = part
        top = jnp.max(part.reshape(CHUNK // 8, 8, COLS), axis=0)
        return top if peak is None else jnp.maximum(peak, top)

    def score_fresh(index, weights, new, peak):
        part = score(fresh_keys[...], weights)
        number = fresh_packed[...]
        latest = jnp.zeros((1, COLS), jnp.int32)
        for b in range(TILE_BLOCKS):
            latest = jnp.where(lane // BLOCK == b, entry(index, b) // NBLOCKS, latest)
        latest = latest * BLOCK + lane % BLOCK
        allowed = (number >= tile_first[index]) & (number <= latest)
        part = jnp.where(allowed, part, NEG)
        new[...] = part
        return jnp.maximum(peak, jnp.max(part.reshape(FRESH // 8, 8, COLS), axis=0))

    def weigh(part, top):
        p = jnp.exp2(part - top)
        high, low = split(p)
        return jnp.sum(p.reshape(part.shape[0] // 8, 8, COLS), axis=0), high, low

    def accumulate(value, high, low, acc):
        first = jnp.dot(value, high, preferred_element_type=jnp.float32)
        second = jnp.dot(value[0:HD], low, preferred_element_type=jnp.float32)
        both = first[0:HD] + first[HD : 2 * HD] + second
        return both if acc is None else acc + both

    def finish(index):
        done = ready[...].T.reshape(TILE, HEADS, HD)
        level = jnp.broadcast_to(ready_level[0:1], (HD, COLS)).T.reshape(TILE, HEADS, HD)
        req = tile_req[index]
        carry[req, 0] = done
        carry[req, 1] = level
        for b in range(TILE_BLOCKS):
            put_block(
                entry(index, b), tile_first[index], tile_end[index],
                lambda u: done[b * BLOCK + u], lambda u: level[b * BLOCK + u],
            )

    def step(now, follow, mine, other):
        weights_now, scores_now, new_now, peak_now = mine
        weights_later, scores_later, new_later, peak_later = other
        finish(jnp.maximum(now - 1, 0))
        later = now + 1
        top = jnp.max(peak_now[...], axis=0, keepdims=True)
        mass, high, low = weigh(new_now[...], top)
        acc = accumulate(fresh_values[...], high, low, None)
        peak = None
        for c in range(CHUNKS):
            if follow:
                peak = score_chunk(later, c, weights_later, scores_later, peak)
            more, high, low = weigh(scores_now[pl.ds(c * CHUNK, CHUNK), :], top)
            mass = mass + more
            acc = accumulate(
                values[c // HALF_CHUNKS][tile_req[now], :, pl.ds(c % HALF_CHUNKS * CHUNK, CHUNK)],
                high, low, acc,
            )
        if follow:
            peak_later[...] = score_fresh(later, weights_later, new_later, peak)
            load(jnp.minimum(now + 2, tiles - 1), weights_now)
        total = jnp.sum(mass, axis=0, keepdims=True)
        ready[...] = acc / total
        ready_level[0:1] = top + jnp.log2(total)

    even = (weights_a, scores_a, new_a, peak_a)
    odd = (weights_b, scores_b, new_b, peak_b)
    ready[...] = jnp.zeros_like(ready)
    ready_level[...] = jnp.zeros_like(ready_level)
    load(0, weights_a)
    load(jnp.clip(tiles - 1, 0, 1), weights_b)
    peak = None
    for c in range(CHUNKS):
        peak = score_chunk(0, c, weights_a, scores_a, peak)
    peak_a[...] = score_fresh(0, weights_a, new_a, peak)

    def pair(j, _):
        for this, (a, b) in enumerate(((even, odd), (odd, even))):
            current = 2 * j + this

            @pl.when(current < tiles - 1)
            def _():
                step(current, True, a, b)

            @pl.when(current == tiles - 1)
            def _():
                step(current, False, a, b)

        return 0

    lax.fori_loop(0, (tiles + 1) // 2, pair, 0)

    @pl.when(tiles > 0)
    def _():
        finish(tiles - 1)

    for index, target in enumerate(outs):
        target[...] = out[pl.ds(2 * index, 2)]


def attend(group, table, carry, pieces, fresh, keys, values):
    n_out = len(GROUPS[group])
    carried = [] if carry is None else [carry]
    n_vmem = len(pieces) + 7 + len(carried)
    hold = jax.ShapeDtypeStruct((REQS, 2, TILE, HEADS, HD), jnp.float32)
    table_out = [jax.ShapeDtypeStruct((LENGTHS + REQS,), jnp.int32)]
    slots = 2 * n_out
    tile_table = pltpu.SMEM((MAX_TILES,), jnp.int32)
    return pl.pallas_call(
        functools.partial(attend_kernel, group, n_out),
        in_specs=[SMEM] + [VMEM] * n_vmem,
        out_specs=[VMEM] * n_out + [SMEM] * (group == 0) + [VMEM],
        out_shape=[jax.ShapeDtypeStruct((2, SLOT_TOK + 1, HEADS, HD), jnp.float32)] * n_out
        + table_out * (group == 0)
        + [hold],
        scratch_shapes=[
            pltpu.VMEM((len(pieces) * 2 * PART, HEADS, HD), jnp.float32),
            pltpu.VMEM((slots + 1, SLOT_TOK + 1, HEADS, HD), jnp.float32),
            pltpu.VMEM((COLS, 3 * HD), jnp.bfloat16),
            pltpu.VMEM((COLS, 3 * HD), jnp.bfloat16),
            pltpu.VMEM((COLS, HD), jnp.float32),
            pltpu.VMEM((POSITIONS, COLS), jnp.float32),
            pltpu.VMEM((POSITIONS, COLS), jnp.float32),
            pltpu.VMEM((FRESH, COLS), jnp.float32),
            pltpu.VMEM((FRESH, COLS), jnp.float32),
            pltpu.VMEM((8, COLS), jnp.float32),
            pltpu.VMEM((8, COLS), jnp.float32),
            pltpu.VMEM((HD, COLS), jnp.float32),
            pltpu.VMEM((8, COLS), jnp.float32),
        ]
        + [tile_table] * 5
        + [
            pltpu.VMEM((4 * len(REACH), HD), jnp.int32),
            pltpu.SMEM((4 * len(REACH), HD), jnp.int32),
            pltpu.SemaphoreType.DMA,
        ]
        * (group == 0),
        compiler_params=pltpu.CompilerParams(vmem_limit_bytes=16 << 20),
        cost_estimate=pl.CostEstimate(
            flops=n_out * 8 * 10**9, bytes_accessed=8 << 20, transcendentals=10**6
        ),
        name="attend",
    )(table, *carried, *pieces, *fresh, *keys, *values)


def blend(parts, store, store_level=None):
    levels = [part[SLOT_TOK] for part in parts]
    top = levels[0]
    for level in levels[1:]:
        top = jnp.maximum(top, level)
    shares = [jnp.exp2(level - top) for level in levels]
    total = shares[0]
    for share in shares[1:]:
        total = total + share
    shares = [share / total for share in shares]
    for t in range(SLOT_TOK):
        acc = parts[0][t] * shares[0][:, t : t + 1]
        for part, share in zip(parts[1:], shares[1:]):
            acc = acc + part[t] * share[:, t : t + 1]
        store(t, acc)
    if store_level is not None:
        store_level(top + jnp.log2(total))


def put(ref, slot, t, value):
    ref[slot, t] = value


def hop_kernel(*refs):
    n = len(refs) // 3
    for part, got, out in zip(refs[:n], refs[n : 2 * n], refs[2 * n :]):
        for slot in range(2):
            store = functools.partial(put, out, slot)
            blend((part.at[slot], got.at[slot]), store, functools.partial(store, SLOT_TOK))


def hop(parts, got):
    n = len(parts)
    return pl.pallas_call(
        hop_kernel,
        in_specs=[VMEM] * (2 * n),
        out_specs=[VMEM] * n,
        out_shape=[jax.ShapeDtypeStruct(parts[0].shape, jnp.float32)] * n,
        compiler_params=pltpu.CompilerParams(vmem_limit_bytes=4 << 20),
        name="hop",
    )(*parts, *got)


def arrive_kernel(corner, own, up_in, down_in, out):
    pair = TOK // HEADS
    for slot in range(2):
        def store(t, value, slot=slot):
            target = jnp.bitwise_xor(corner[0], 2 * slot + t // TOK)
            inside = t % TOK
            out[target, inside // pair, inside % pair] = value

        def store_level(level, slot=slot):
            for half in range(2):
                target = jnp.bitwise_xor(corner[0], 2 * slot + half)
                for h in range(HEADS):
                    first = half * TOK + h * pair
                    out[target, h, pair] = jnp.concatenate(
                        [level[:, first : first + pair], jnp.zeros((HEADS, HD - pair), jnp.float32)],
                        axis=1,
                    )

        blend((own.at[slot], up_in.at[slot], down_in.at[slot]), store, store_level)


def arrive(corner, own, up_in, down_in):
    return pl.pallas_call(
        arrive_kernel,
        in_specs=[SMEM] + [VMEM] * 3,
        out_specs=VMEM,
        out_shape=jax.ShapeDtypeStruct((4, HEADS, TOK // HEADS + 1, HEADS, HD), jnp.float32),
        compiler_params=pltpu.CompilerParams(vmem_limit_bytes=4 << 20),
        name="arrive",
    )(corner, own, up_in, down_in)


def settle_kernel(parts, out):
    pair = TOK // HEADS
    for core in range(2):
        for h in range(HEADS):
            one, two = parts.at[core, h], parts.at[2 + core, h]
            levels = (one[pair], two[pair])
            top = jnp.maximum(*levels)
            shares = [jnp.exp2(level - top) for level in levels]
            total = shares[0] + shares[1]
            for t in range(pair):
                value = one[t] * (shares[0] / total)[:, t : t + 1]
                value = value + two[t] * (shares[1] / total)[:, t : t + 1]
                out[t, pl.ds((2 * h + core) * HEADS, HEADS), :] = value


def settle(parts):
    return pl.pallas_call(
        settle_kernel,
        in_specs=[VMEM],
        out_specs=VMEM,
        out_shape=jax.ShapeDtypeStruct((TOK // HEADS, 2 * HEADS * HEADS, HD), jnp.float32),
        compiler_params=pltpu.CompilerParams(vmem_limit_bytes=4 << 20),
        name="settle",
    )(parts)


def pack_kernel(core, plan, queries, mine, theirs):
    for out, half in ((mine, core[0]), (theirs, 1 - core[0])):
        out[0:TOK] = queries[:, pl.ds(pl.multiple_of(half * HEADS, HEADS), HEADS), :]
        lanes = lax.broadcasted_iota(jnp.int32, (HEADS, HD), 1)
        number = jnp.zeros((HEADS, HD), jnp.int32)
        for b in range(TOK // BLOCK):
            number = jnp.where(lanes == b, plan[b], number)
        out[TOK] = number.astype(jnp.float32)


def pack(core, plan, queries):
    return pl.pallas_call(
        pack_kernel,
        in_specs=[SMEM, SMEM, VMEM],
        out_specs=[VMEM] * 2,
        out_shape=[jax.ShapeDtypeStruct((PART, HEADS, HD), jnp.float32)] * 2,
        compiler_params=pltpu.CompilerParams(vmem_limit_bytes=2 << 20),
        name="pack",
    )(core, plan, queries)


def body(queries, new_kv, cache_keys, cache_values, new_lengths, block_plan):
    me = lax.axis_index("ctx")
    core = me % 2
    corner = (me % 4).reshape(1)
    n_ctx = 32
    n_head = 8

    def send(x, target):
        return lax.ppermute(x, "ctx", [(i, target(i)) for i in range(n_ctx)])

    def across(i):
        return i ^ 1

    def beside(i):
        return i ^ 2

    def along(k):
        return lambda i: (i + 4 * k) % n_ctx

    up, down = along(1), along(-1)
    tie = lax.optimization_barrier

    mine, theirs = pack(core.reshape(1), block_plan, queries.reshape(TOK, 2 * HEADS, HD))
    near = {0: jnp.concatenate([mine, send(theirs, across)])}
    corner, near[0], cache_keys, cache_values = tie((corner, near[0], cache_keys, cache_values))
    near[-1], near[1] = send(near[0], up), send(near[0], down)
    far = {0: send(near[0], beside)}
    other_k, other_v = send(cache_keys, across), send(cache_values, across)
    fresh = new_kv[:, :, 0]
    fresh_other = send(fresh, across)
    own_half = list(prepare(cache_keys[:, :, 0], cache_values[:, :, 0]))
    far[0], own_half[0] = tie((far[0], own_half[0]))
    far[-1], far[1] = send(far[0], up), send(far[0], down)
    for held in (near, far):
        held[-2], held[2] = send(held[-1], up), send(held[1], down)
    *other_half, fresh_keys, fresh_values, fresh_packed = prepare(
        other_k[:, :, 0], other_v[:, :, 0], fresh, fresh_other, near[0]
    )
    fresh = (fresh_keys, fresh_values, fresh_packed)
    near[-2], other_half[0] = tie((near[-2], other_half[0]))
    for held in (near, far):
        held[-3], held[3] = send(held[-2], up), send(held[2], down)
    near[4], far[4] = send(near[-3], up), send(far[3], down)
    keys, values = zip(own_half, other_half)

    def call(group, table, carry):
        pieces = [held[k] for k in REACH[GROUPS[group][0] :] for held in (near, far)]
        return attend(group, table, carry, pieces, fresh, keys, values)

    part, table, carry = call(0, new_lengths, None)
    carry, part = tie((carry, part))
    got = (send(part, up),)
    for group in range(1, 4):
        up_part, down_part, carry = call(group, table, carry)
        if group == 1:
            sent = (*hop((up_part,), got), down_part)
        else:
            sent = hop((up_part, down_part), got)
        carry, *sent = tie((carry, *sent))
        got = (send(sent[0], up), send(sent[1], down))
    own, _ = call(4, table, carry)
    parts = arrive(corner, own, *got)
    plane = 4 * n_head
    home = lax.all_to_all(
        parts.reshape((plane,) + parts.shape[2:]), ("ctx", "head"),
        split_axis=0, concat_axis=0, tiled=True,
        axis_index_groups=[[z * plane + i for i in range(plane)] for z in range(n_ctx // 4)],
    )
    return settle(home.reshape(parts.shape)).reshape(TOK // n_head, n_head * 2 * HEADS * HD)


def solution(mesh):
    placed = (
        P("ctx", "head", None),
        P(None, "ctx", "head", None),
        P(None, "ctx", "head", None),
        P(None, "ctx", "head", None),
        P(),
        P("ctx"),
    )
    return jax.shard_map(
        body, mesh=mesh, in_specs=placed, out_specs=P(("ctx", "head"), None), check_vma=False
    )
```

```python
import functools
import math

import jax
import jax.numpy as jnp
from jax import lax
from jax.experimental import pallas as pl
from jax.experimental.pallas import tpu as pltpu
from jax.sharding import PartitionSpec as P

REQS = 4
HD = 128
HEADS = 8
TOK = 16
BLOCK = 4
TILE = 32
COLS = TILE * HEADS
POSITIONS = 2048
HALF = POSITIONS // 2
CHUNK = 512
CHUNKS = POSITIONS // CHUNK
HALF_CHUNKS = CHUNKS // 2
FRESH = 2 * TOK
SLOT_TOK = 2 * TOK
PART = TOK + 1
MEMBER_BLOCKS = 4 * TOK // BLOCK
NBLOCKS = 8 * MEMBER_BLOCKS
TILE_BLOCKS = TILE // BLOCK
MAX_TILES = 12
REACH = (4, 3, -3, 2, -2, 1, -1, 0)
GROUPS = ((0,), (1, 2), (3, 4), (5, 6), (7,))
ROOM = 64
LAST = (len(GROUPS) - 1) * REQS
SUMS = REQS * ROOM
LENGTHS = SUMS + LAST + REQS
VMEM = pl.BlockSpec(memory_space=pltpu.VMEM)
SMEM = pl.BlockSpec(memory_space=pltpu.SMEM)
NEG = -1e30
SCALE = HD ** (-0.5) * math.log2(math.e)
NT = (((1,), (1,)), ((), ()))


def split(x):
    high = x.astype(jnp.bfloat16)
    low = (x - high.astype(jnp.float32)).astype(jnp.bfloat16)
    return high, low


def prepare_kernel(k, v, *refs):
    keys, values = refs[-2:] if len(refs) == 2 else refs[3:5]
    high, low = split(k[0])
    keys[0, :, 0:HD] = high
    keys[0, :, HD : 2 * HD] = low
    high, low = split(v[0].T)
    values[0, 0:HD] = high
    values[0, HD : 2 * HD] = low
    if len(refs) == 2:
        return
    fresh_own, got, message = refs[:3]
    fresh_keys, fresh_values, fresh_packed = refs[5:]

    @pl.when(pl.program_id(0) == 0)
    def _():
        fresh_other = [
            jnp.concatenate([got[PART + 2 * i], got[PART + 2 * i + 1]], axis=0) for i in range(2)
        ]
        for half, fresh in enumerate((fresh_own, fresh_other)):
            span = pl.ds(half * TOK, TOK)
            high, low = split(fresh[0])
            fresh_keys[span, 0:HD] = high
            fresh_keys[span, HD : 2 * HD] = low
            plan = message[half * PART + TOK].astype(jnp.int32)
            for u in range(TOK):
                block = plan[0:1, u // BLOCK : u // BLOCK + 1]
                fresh_packed[half * TOK + u : half * TOK + u + 1, :] = jnp.broadcast_to(
                    block * BLOCK + u % BLOCK, (1, COLS)
                )
        high, low = split(jnp.concatenate([fresh_own[1], fresh_other[1]], axis=0).T)
        fresh_values[0:HD] = high
        fresh_values[HD : 2 * HD] = low


def prepare(k, v, *fresh):
    def whole(*shape):
        return pl.BlockSpec(shape, lambda r: (0,) * len(shape))

    source = pl.BlockSpec((1, HALF, HD), lambda r: (r, 0, 0))
    shapes = [(REQS, HALF, 2 * HD), (REQS, 2 * HD, HALF)]
    blocks = [pl.BlockSpec((1,) + shape[1:], lambda r: (r, 0, 0)) for shape in shapes]
    kinds = [jnp.bfloat16] * 2
    if fresh:
        extra = [(FRESH, 2 * HD), (2 * HD, FRESH), (FRESH, COLS)]
        shapes += extra
        blocks += [whole(*shape) for shape in extra]
        kinds += [jnp.bfloat16, jnp.bfloat16, jnp.int32]
    return pl.pallas_call(
        prepare_kernel,
        grid=(REQS,),
        in_specs=[source] * 2 + [whole(*x.shape) for x in fresh],
        out_specs=blocks,
        out_shape=[jax.ShapeDtypeStruct(*pair) for pair in zip(shapes, kinds)],
        compiler_params=pltpu.CompilerParams(vmem_limit_bytes=8 << 20),
        cost_estimate=pl.CostEstimate(flops=10**7, bytes_accessed=8 << 20, transcendentals=0),
        name="prepare",
    )(k, v, *fresh)


def build_lists(lengths, plan, table):
    bounds = [jnp.int32(0)]
    for req in range(REQS):
        table[LENGTHS + req] = lengths[req]
        bounds.append(bounds[-1] + lengths[req])
    counts = (jnp.int32(0),) * REQS
    for group, members in enumerate(GROUPS):
        first = members[0] * MEMBER_BLOCKS

        def sort_block(j, counts):
            block = plan[j // BLOCK, lax.rem(j, BLOCK)]
            value = block * NBLOCKS + j
            low = block * BLOCK
            new = []
            for req in range(REQS):
                table[req * ROOM + counts[req]] = value
                inside = (low + BLOCK > bounds[req]) & (low < bounds[req + 1])
                new.append(counts[req] + inside.astype(jnp.int32))
            return tuple(new)

        counts = lax.fori_loop(
            first, first + len(members) * MEMBER_BLOCKS, sort_block, counts, unroll=4
        )
        for req in range(REQS):
            table[SUMS + group * REQS + req] = counts[req]


def attend_kernel(group, n_out, *refs):
    first_member = GROUPS[group][0]
    n_pieces = 2 * (len(REACH) - first_member)
    slots = 2 * len(GROUPS[group])
    first_block = first_member * MEMBER_BLOCKS
    if group == 0:
        lengths, refs = refs[0], refs[1:]
    else:
        table_in, held, refs = refs[0], refs[1], refs[2:]
    pieces, refs = refs[:n_pieces], refs[n_pieces:]
    fresh_keys, fresh_values, fresh_packed = refs[:3]
    keys, values, refs = refs[3:5], refs[5:7], refs[7:]
    outs, refs = refs[:n_out], refs[n_out:]
    if group == 0:
        table, refs = refs[0], refs[1:]
        numbers, plan, sem = refs[-3:]
        refs = refs[:-3]
    else:
        table, sem = refs[-2:]
        refs = refs[:-2]
        copy = pltpu.make_async_copy(table_in, table, sem)
        copy.start()
    carry, refs = refs[0], refs[1:]
    (
        queries, out, weights_a, weights_b, rows, scores_a, scores_b, new_a, new_b,
        peak_a, peak_b, ready, ready_level,
        tile_req, tile_first, tile_end, tile_place, tile_last,
    ) = refs

    if group == 0:
        for index, piece in enumerate(pieces):
            for part in range(2):
                row = 2 * index + part
                numbers[row : row + 1] = piece[part * PART + TOK, 0:1].astype(jnp.int32)
        copy = pltpu.make_async_copy(numbers, plan, sem)
        copy.start()
    for index, piece in enumerate(pieces):
        queries[pl.ds(index * 2 * PART, 2 * PART)] = piece[...]
    for slot in range(slots):
        out[slot, SLOT_TOK] = jnp.zeros((HEADS, HD), jnp.float32)
    if group == 0:
        copy.wait()
        build_lists(lengths, plan, table)
    else:
        copy.wait()

    lane = lax.broadcasted_iota(jnp.int32, (1, COLS), 1) // HEADS
    lanes = lax.broadcasted_iota(jnp.int32, (HEADS, HD), 1)

    def put_block(entry, begin, end, value, level):
        block = entry // NBLOCKS
        local = lax.rem(entry, NBLOCKS) - first_block
        mine = local < slots * SLOT_TOK // BLOCK
        slot = local // (SLOT_TOK // BLOCK)
        base = lax.rem(local, SLOT_TOK // BLOCK) * BLOCK
        for u in range(BLOCK):
            number = block * BLOCK + u
            good = mine & (number >= begin) & (number < end)
            where = jnp.where(good, slot, slots)
            out[where, base + u] = value(u)
            out[where, SLOT_TOK] = jnp.where(
                lanes == base + u, level(u), out[where, SLOT_TOK]
            )

    begin = jnp.int32(0)
    tiles = jnp.int32(0)
    tile_req[0] = 0
    tile_first[0] = 0
    tile_end[0] = 1
    tile_place[0] = 0
    tile_last[0] = 0
    for req in range(REQS):
        end = begin + table[LENGTHS + req]
        count = table[SUMS + group * REQS + req]
        total = table[SUMS + LAST + req]
        upto = (count + TILE_BLOCKS - 1) // TILE_BLOCKS
        done = jnp.int32(0)
        if group > 0:
            before = table[SUMS + (group - 1) * REQS + req]
            done = (before + TILE_BLOCKS - 1) // TILE_BLOCKS

            def reuse(p, _, req=req, begin=begin, end=end, done=done):
                place = (p - (done - 1) * TILE_BLOCKS) * BLOCK
                put_block(
                    table[req * ROOM + p], begin, end,
                    lambda u: held[req, 0, place + u], lambda u: held[req, 1, place + u],
                )
                return 0

            lax.fori_loop(before, jnp.minimum(count, done * TILE_BLOCKS), reuse, 0)
            carry[req] = held[req]

        def list_tile(t, _, req=req, begin=begin, end=end, tiles=tiles, done=done, total=total):
            tile_req[tiles + t - done] = req
            tile_first[tiles + t - done] = begin
            tile_end[tiles + t - done] = end
            tile_place[tiles + t - done] = req * ROOM + t * TILE_BLOCKS
            tile_last[tiles + t - done] = req * ROOM + total - 1
            return 0

        lax.fori_loop(done, upto, list_tile, 0)
        begin = end
        tiles = tiles + upto - done

    def entry(index, b):
        return table[jnp.minimum(tile_place[index] + b, tile_last[index])]

    def load(index, weights):
        for b in range(TILE_BLOCKS):
            local = jnp.maximum(lax.rem(entry(index, b), NBLOCKS) - first_block, 0)
            row = local // BLOCK * PART + lax.rem(local, BLOCK) * BLOCK
            for u in range(BLOCK):
                rows[pl.ds((b * BLOCK + u) * HEADS, HEADS), :] = queries[row + u]
        high, low = split(rows[...] * SCALE)
        weights[:, 0:HD] = high
        weights[:, HD : 2 * HD] = high
        weights[:, 2 * HD : 3 * HD] = low

    def score(key, weights):
        both = lax.dot_general(
            key, weights[:, 0 : 2 * HD], NT, preferred_element_type=jnp.float32
        )
        return both + lax.dot_general(
            key[:, 0:HD], weights[:, 2 * HD : 3 * HD], NT, preferred_element_type=jnp.float32
        )

    def score_chunk(index, c, weights, scores, peak):
        part = score(
            keys[c // HALF_CHUNKS][tile_req[index], pl.ds(c % HALF_CHUNKS * CHUNK, CHUNK), :],
            weights,
        )
        scores[pl.ds(c * CHUNK, CHUNK), :] = part
        top = jnp.max(part.reshape(CHUNK // 8, 8, COLS), axis=0)
        return top if peak is None else jnp.maximum(peak, top)

    def score_fresh(index, weights, new, peak):
        part = score(fresh_keys[...], weights)
        number = fresh_packed[...]
        latest = jnp.zeros((1, COLS), jnp.int32)
        for b in range(TILE_BLOCKS):
            latest = jnp.where(lane // BLOCK == b, entry(index, b) // NBLOCKS, latest)
        latest = latest * BLOCK + lane % BLOCK
        allowed = (number >= tile_first[index]) & (number <= latest)
        part = jnp.where(allowed, part, NEG)
        new[...] = part
        return jnp.maximum(peak, jnp.max(part.reshape(FRESH // 8, 8, COLS), axis=0))

    def weigh(part, top):
        p = jnp.exp2(part - top)
        high, low = split(p)
        return jnp.sum(p.reshape(part.shape[0] // 8, 8, COLS), axis=0), high, low

    def accumulate(value, high, low, acc):
        first = jnp.dot(value, high, preferred_element_type=jnp.float32)
        second = jnp.dot(value[0:HD], low, preferred_element_type=jnp.float32)
        both = first[0:HD] + first[HD : 2 * HD] + second
        return both if acc is None else acc + both

    def finish(index):
        done = ready[...].T.reshape(TILE, HEADS, HD)
        level = jnp.broadcast_to(ready_level[0:1], (HD, COLS)).T.reshape(TILE, HEADS, HD)
        req = tile_req[index]
        carry[req, 0] = done
        carry[req, 1] = level
        for b in range(TILE_BLOCKS):
            put_block(
                entry(index, b), tile_first[index], tile_end[index],
                lambda u: done[b * BLOCK + u], lambda u: level[b * BLOCK + u],
            )

    def step(now, follow, mine, other):
        weights_now, scores_now, new_now, peak_now = mine
        weights_later, scores_later, new_later, peak_later = other
        finish(jnp.maximum(now - 1, 0))
        later = now + 1
        top = jnp.max(peak_now[...], axis=0, keepdims=True)
        mass, high, low = weigh(new_now[...], top)
        acc = accumulate(fresh_values[...], high, low, None)
        peak = None
        for c in range(CHUNKS):
            if follow:
                peak = score_chunk(later, c, weights_later, scores_later, peak)
            more, high, low = weigh(scores_now[pl.ds(c * CHUNK, CHUNK), :], top)
            mass = mass + more
            acc = accumulate(
                values[c // HALF_CHUNKS][tile_req[now], :, pl.ds(c % HALF_CHUNKS * CHUNK, CHUNK)],
                high, low, acc,
            )
        if follow:
            peak_later[...] = score_fresh(later, weights_later, new_later, peak)
            load(jnp.minimum(now + 2, tiles - 1), weights_now)
        total = jnp.sum(mass, axis=0, keepdims=True)
        ready[...] = acc / total
        ready_level[0:1] = top + jnp.log2(total)

    even = (weights_a, scores_a, new_a, peak_a)
    odd = (weights_b, scores_b, new_b, peak_b)
    ready[...] = jnp.zeros_like(ready)
    ready_level[...] = jnp.zeros_like(ready_level)
    load(0, weights_a)
    load(jnp.clip(tiles - 1, 0, 1), weights_b)
    peak = None
    for c in range(CHUNKS):
        peak = score_chunk(0, c, weights_a, scores_a, peak)
    peak_a[...] = score_fresh(0, weights_a, new_a, peak)

    def pair(j, _):
        for this, (a, b) in enumerate(((even, odd), (odd, even))):
            current = 2 * j + this

            @pl.when(current < tiles - 1)
            def _():
                step(current, True, a, b)

            @pl.when(current == tiles - 1)
            def _():
                step(current, False, a, b)

        return 0

    lax.fori_loop(0, (tiles + 1) // 2, pair, 0)

    @pl.when(tiles > 0)
    def _():
        finish(tiles - 1)

    for index, target in enumerate(outs):
        target[...] = out[pl.ds(2 * index, 2)]


def attend(group, table, carry, pieces, fresh, keys, values):
    n_out = len(GROUPS[group])
    carried = [] if carry is None else [carry]
    n_vmem = len(pieces) + 7 + len(carried)
    hold = jax.ShapeDtypeStruct((REQS, 2, TILE, HEADS, HD), jnp.float32)
    table_out = [jax.ShapeDtypeStruct((LENGTHS + REQS,), jnp.int32)]
    slots = 2 * n_out
    tile_table = pltpu.SMEM((MAX_TILES,), jnp.int32)
    return pl.pallas_call(
        functools.partial(attend_kernel, group, n_out),
        in_specs=[SMEM if group == 0 else VMEM] + [VMEM] * n_vmem,
        out_specs=[VMEM] * n_out + [SMEM] * (group == 0) + [VMEM],
        out_shape=[jax.ShapeDtypeStruct((2, SLOT_TOK + 1, HEADS, HD), jnp.float32)] * n_out
        + table_out * (group == 0)
        + [hold],
        scratch_shapes=[
            pltpu.VMEM((len(pieces) * 2 * PART, HEADS, HD), jnp.float32),
            pltpu.VMEM((slots + 1, SLOT_TOK + 1, HEADS, HD), jnp.float32),
            pltpu.VMEM((COLS, 3 * HD), jnp.bfloat16),
            pltpu.VMEM((COLS, 3 * HD), jnp.bfloat16),
            pltpu.VMEM((COLS, HD), jnp.float32),
            pltpu.VMEM((POSITIONS, COLS), jnp.float32),
            pltpu.VMEM((POSITIONS, COLS), jnp.float32),
            pltpu.VMEM((FRESH, COLS), jnp.float32),
            pltpu.VMEM((FRESH, COLS), jnp.float32),
            pltpu.VMEM((8, COLS), jnp.float32),
            pltpu.VMEM((8, COLS), jnp.float32),
            pltpu.VMEM((HD, COLS), jnp.float32),
            pltpu.VMEM((8, COLS), jnp.float32),
        ]
        + [tile_table] * 5
        + (
            [
                pltpu.VMEM((4 * len(REACH), HD), jnp.int32),
                pltpu.SMEM((4 * len(REACH), HD), jnp.int32),
            ]
            if group == 0
            else [pltpu.SMEM((LENGTHS + REQS,), jnp.int32)]
        )
        + [pltpu.SemaphoreType.DMA],
        compiler_params=pltpu.CompilerParams(vmem_limit_bytes=16 << 20),
        cost_estimate=pl.CostEstimate(
            flops=n_out * 8 * 10**9, bytes_accessed=8 << 20, transcendentals=10**6
        ),
        name="attend",
    )(table, *carried, *pieces, *fresh, *keys, *values)


def blend(parts, store, store_level=None):
    levels = [part[SLOT_TOK] for part in parts]
    top = levels[0]
    for level in levels[1:]:
        top = jnp.maximum(top, level)
    shares = [jnp.exp2(level - top) for level in levels]
    total = shares[0]
    for share in shares[1:]:
        total = total + share
    shares = [share / total for share in shares]
    for t in range(SLOT_TOK):
        acc = parts[0][t] * shares[0][:, t : t + 1]
        for part, share in zip(parts[1:], shares[1:]):
            acc = acc + part[t] * share[:, t : t + 1]
        store(t, acc)
    if store_level is not None:
        store_level(top + jnp.log2(total))


def put(ref, slot, t, value):
    ref[slot, t] = value


def hop_kernel(*refs):
    n = len(refs) // 3
    for part, got, out in zip(refs[:n], refs[n : 2 * n], refs[2 * n :]):
        for slot in range(2):
            store = functools.partial(put, out, slot)
            blend((part.at[slot], got.at[slot]), store, functools.partial(store, SLOT_TOK))


def hop(parts, got):
    n = len(parts)
    return pl.pallas_call(
        hop_kernel,
        in_specs=[VMEM] * (2 * n),
        out_specs=[VMEM] * n,
        out_shape=[jax.ShapeDtypeStruct(parts[0].shape, jnp.float32)] * n,
        compiler_params=pltpu.CompilerParams(vmem_limit_bytes=4 << 20),
        name="hop",
    )(*parts, *got)


def arrive_kernel(corner, own, up_in, down_in, out):
    pair = TOK // HEADS
    for slot in range(2):
        def store(t, value, slot=slot):
            target = jnp.bitwise_xor(corner[0], 2 * slot + t // TOK)
            inside = t % TOK
            out[target, inside // pair, inside % pair] = value

        def store_level(level, slot=slot):
            for half in range(2):
                target = jnp.bitwise_xor(corner[0], 2 * slot + half)
                for h in range(HEADS):
                    first = half * TOK + h * pair
                    out[target, h, pair] = jnp.concatenate(
                        [level[:, first : first + pair], jnp.zeros((HEADS, HD - pair), jnp.float32)],
                        axis=1,
                    )

        blend((own.at[slot], up_in.at[slot], down_in.at[slot]), store, store_level)


def arrive(corner, own, up_in, down_in):
    return pl.pallas_call(
        arrive_kernel,
        in_specs=[SMEM] + [VMEM] * 3,
        out_specs=VMEM,
        out_shape=jax.ShapeDtypeStruct((4, HEADS, TOK // HEADS + 1, HEADS, HD), jnp.float32),
        compiler_params=pltpu.CompilerParams(vmem_limit_bytes=4 << 20),
        name="arrive",
    )(corner, own, up_in, down_in)


def settle_kernel(parts, out):
    pair = TOK // HEADS
    for core in range(2):
        for h in range(HEADS):
            one, two = parts.at[core, h], parts.at[2 + core, h]
            levels = (one[pair], two[pair])
            top = jnp.maximum(*levels)
            shares = [jnp.exp2(level - top) for level in levels]
            total = shares[0] + shares[1]
            for t in range(pair):
                value = one[t] * (shares[0] / total)[:, t : t + 1]
                value = value + two[t] * (shares[1] / total)[:, t : t + 1]
                for j in range(HEADS):
                    first = ((2 * h + core) * HEADS + j) * HD
                    out[t : t + 1, first : first + HD] = value[j : j + 1]


def settle(parts):
    return pl.pallas_call(
        settle_kernel,
        in_specs=[VMEM],
        out_specs=VMEM,
        out_shape=jax.ShapeDtypeStruct((TOK // HEADS, 2 * HEADS * HEADS * HD), jnp.float32),
        compiler_params=pltpu.CompilerParams(vmem_limit_bytes=4 << 20),
        name="settle",
    )(parts)


def pack_kernel(core, plan, queries, fresh, mine, theirs):
    for index in range(4):
        first = index % 2 * HEADS
        theirs[PART + index] = fresh[index // 2, first : first + HEADS]
    for out, half in ((mine, core[0]), (theirs, 1 - core[0])):
        out[0:TOK] = queries[:, pl.ds(pl.multiple_of(half * HEADS, HEADS), HEADS), :]
        lanes = lax.broadcasted_iota(jnp.int32, (HEADS, HD), 1)
        number = jnp.zeros((HEADS, HD), jnp.int32)
        for b in range(TOK // BLOCK):
            number = jnp.where(lanes == b, plan[b], number)
        out[TOK] = number.astype(jnp.float32)


def pack(core, plan, queries, fresh):
    return pl.pallas_call(
        pack_kernel,
        in_specs=[SMEM, SMEM, VMEM, VMEM],
        out_specs=[VMEM] * 2,
        out_shape=[
            jax.ShapeDtypeStruct((rows, HEADS, HD), jnp.float32) for rows in (PART, PART + 4)
        ],
        compiler_params=pltpu.CompilerParams(vmem_limit_bytes=2 << 20),
        name="pack",
    )(core, plan, queries, fresh)


def body(queries, new_kv, cache_keys, cache_values, new_lengths, block_plan):
    me = lax.axis_index("ctx")
    core = me % 2
    corner = (me % 4).reshape(1)
    n_ctx = 32
    n_head = 8

    def send(x, target):
        return lax.ppermute(x, "ctx", [(i, target(i)) for i in range(n_ctx)])

    def across(i):
        return i ^ 1

    def beside(i):
        return i ^ 2

    def along(k):
        return lambda i: (i + 4 * k) % n_ctx

    up, down = along(1), along(-1)
    tie = lax.optimization_barrier

    fresh = new_kv[:, :, 0]
    mine, theirs = pack(
        core.reshape(1), block_plan, queries.reshape(TOK, 2 * HEADS, HD), fresh
    )
    got = send(theirs, across)
    near = {0: jnp.concatenate([mine, got[:PART]])}
    corner, near[0], cache_keys, cache_values = tie((corner, near[0], cache_keys, cache_values))
    near[-1], near[1] = send(near[0], up), send(near[0], down)
    far = {0: send(near[0], beside)}
    other_k, other_v = send(cache_keys, across), send(cache_values, across)
    own_half = list(prepare(cache_keys[:, :, 0], cache_values[:, :, 0]))
    far[0], own_half[0] = tie((far[0], own_half[0]))
    far[-1], far[1] = send(far[0], up), send(far[0], down)
    for held in (near, far):
        held[-2], held[2] = send(held[-1], up), send(held[1], down)
    *other_half, fresh_keys, fresh_values, fresh_packed = prepare(
        other_k[:, :, 0], other_v[:, :, 0], fresh, got, near[0]
    )
    fresh = (fresh_keys, fresh_values, fresh_packed)
    near[-2], other_half[0] = tie((near[-2], other_half[0]))
    for held in (near, far):
        held[-3], held[3] = send(held[-2], up), send(held[2], down)
    near[4], far[4] = send(near[-3], up), send(far[3], down)
    keys, values = zip(own_half, other_half)

    def call(group, table, carry):
        pieces = [held[k] for k in REACH[GROUPS[group][0] :] for held in (near, far)]
        return attend(group, table, carry, pieces, fresh, keys, values)

    part, table, carry = call(0, new_lengths, None)
    carry, part = tie((carry, part))
    got = (send(part, up),)
    for group in range(1, 4):
        up_part, down_part, carry = call(group, table, carry)
        if group == 1:
            sent = (*hop((up_part,), got), down_part)
        else:
            sent = hop((up_part, down_part), got)
        carry, *sent = tie((carry, *sent))
        got = (send(sent[0], up), send(sent[1], down))
    own, _ = call(4, table, carry)
    parts = arrive(corner, own, *got)
    plane = 4 * n_head
    home = lax.all_to_all(
        parts.reshape((plane,) + parts.shape[2:]), ("ctx", "head"),
        split_axis=0, concat_axis=0, tiled=True,
        axis_index_groups=[[z * plane + i for i in range(plane)] for z in range(n_ctx // 4)],
    )
    return settle(home.reshape(parts.shape))


def solution(mesh):
    placed = (
        P("ctx", "head", None),
        P(None, "ctx", "head", None),
        P(None, "ctx", "head", None),
        P(None, "ctx", "head", None),
        P(),
        P("ctx"),
    )
    return jax.shard_map(
        body, mesh=mesh, in_specs=placed, out_specs=P(("ctx", "head"), None), check_vma=False
    )
```
